512 devices in a mesh: dp: 32 (over z, y_lo), tensor: 4 (over x), precond: 4 (over y_hi, core).
Axes of the slice: x: 4, y: 8 (y_hi: 2, y_lo: 4; y = y_hi * 4 + y_lo), z: 8, core: 2. Of those that a mesh axis runs over, the one named last changes fastest.
Arguments:
- x_in: bfloat16 [4096, 2048], P('dp', 'precond'), may hold values from -12 to 12
- grad_out: bfloat16 [4096, 2048], P('dp', 'tensor'), may hold values from -12 to 12
- weight: bfloat16 [2048, 2048], P('precond', 'tensor'), may hold values from -0.125 to 0.125
Outputs:
- layer_out: bfloat16 [4096, 2048], P('dp', 'tensor')
- grad_in: bfloat16 [4096, 2048], P('dp', 'precond')
- left_root: float32 [4, 512, 2048], P('precond', 'dp', 'tensor')
- right_root: float32 [4, 512, 2048], P('precond', 'dp', 'tensor')
The draws below stay inside these ranges and needn't reach their ends.
All inputs are finite; a program needn't handle non-finite values.
Results may differ from the reference program's by a relative error of at most 0.013.
Values may be sent and summed in bfloat16 or wider, within the bound.
No kernel may reach another device: no remote copies, remote signals or barrier semaphores. Data moves between devices by JAX's collectives and lax.ppermute only.
A program may use at most 64 MiB of HBM per device.

```python
import jax
import jax.numpy as jnp
from jax import lax

D = 2048
E = 2048
BLK = 512
ITERS = 6
TOKENS = 4096


def quantized(values):
    return jnp.floor(values * 32.0 + 0.5) / 32.0


def token_signal(key):
    key = jax.random.fold_in(key, 7)
    normal_key = jax.random.fold_in(key, 0)
    normal_values = jax.random.truncated_normal(normal_key, -3.0, 3.0, (TOKENS, 1), jnp.float32)
    return normal_values


def featured(key, columns, spread, signal):
    scale_key, value_key, place_key = jax.random.split(key, 3)
    column_scale = jnp.exp(jax.random.uniform(scale_key, (1, columns), jnp.float32, -0.6931472, 0.6931472))
    normal_values = jax.random.truncated_normal(value_key, -4.0, 4.0, (TOKENS, columns), jnp.float32)
    values = normal_values
    places = jax.random.randint(place_key, (columns // BLK, 1), 0, BLK)
    offsets = lax.broadcasted_iota(jnp.int32, (columns // BLK, BLK), 1)
    outlier = jnp.where(offsets == places, 1.0, 0.0).astype(jnp.float32).reshape(1, columns)
    total = values * column_scale * spread + signal * outlier
    return quantized(total).astype(jnp.bfloat16)


def draw_x_in(key, part):
    base = key
    key = jax.random.fold_in(key, 11)
    signal = token_signal(base)
    return featured(key, D, 0.45, signal)


def draw_grad_out(key, part):
    base = key
    key = jax.random.fold_in(key, 12)
    signal = token_signal(base)
    return featured(key, E, 0.45, signal)


def block_levels(stream_key, shape, cuts, smallest, top_value):
    gain = 1.0
    for axis_at, parts in cuts:
        steps = jax.random.uniform(jax.random.fold_in(jax.random.fold_in(stream_key, 6), axis_at), (parts,), jnp.float32, smallest / len(cuts), top_value / len(cuts))
        gain = gain * jnp.repeat(jnp.exp(steps), shape[axis_at] // parts).reshape((-1,) + (1,) * (len(shape) - 1 - axis_at))
    return gain


def noise(key, shape, scale, most, cuts=(), kind=jnp.bfloat16):
    drawn = jax.random.normal(key, shape, jnp.float32) * scale
    if len(cuts) > 0:
        drawn = block_levels(key, shape, cuts, -0.22, 0.18) * drawn
    return jnp.clip(drawn, min=-most, max=most).astype(kind)


def setup_inputs(seed: int = 0) -> dict:
    streams_of = jax.random.split(jax.random.key(seed), 4)
    return {
        "x_in": draw_x_in(jax.random.fold_in(streams_of[3], 71), 0),
        "grad_out": draw_grad_out(jax.random.fold_in(streams_of[3], 71), 0),
        "weight": noise(streams_of[2], (D, E), D ** -0.5, 0.125, ((0, 4), (1, 4))),
    }


def product(left, right):
    return jnp.dot(left, right, preferred_element_type=jnp.float32, precision=lax.Precision.HIGHEST)

def inverse_root(statistic):
    extent = statistic.shape[0]
    identity = jnp.eye(extent, dtype=jnp.float32)
    statistic = statistic + 1e-06 * identity
    scaling = 0.4 * jnp.sqrt(jnp.sum(statistic * statistic) + 1e-06)
    moment = statistic / scaling
    inverse = identity * scaling ** (-0.25)
    for iteration in range(ITERS):
        factor = (5.0 * identity - moment) / 4.0
        inverse = product(inverse, factor)
        if iteration + 1 < ITERS:
            moment = product(factor, product(factor, product(factor, product(factor, moment))))
    return inverse

def rounded(values):
    return lax.optimization_barrier(values.astype(jnp.bfloat16)).astype(jnp.float32)

def reference(x_in, grad_out, weight):
    inputs_wide = x_in.astype(jnp.float32)
    upstream = grad_out.astype(jnp.float32)
    weight_wide = weight.astype(jnp.float32)
    layer_sum = jnp.zeros((TOKENS, E), jnp.float32)
    for block_row in range(D // BLK):
        contribution = product(inputs_wide[:, block_row * BLK:(block_row + 1) * BLK], weight_wide[block_row * BLK:(block_row + 1) * BLK, :])
        layer_sum = layer_sum + rounded(contribution)
    layer_out = layer_sum.astype(jnp.bfloat16)
    input_sum = jnp.zeros((TOKENS, D), jnp.float32)
    for block_col in range(E // BLK):
        contribution = product(upstream[:, block_col * BLK:(block_col + 1) * BLK], weight_wide[:, block_col * BLK:(block_col + 1) * BLK].T)
        input_sum = input_sum + rounded(contribution)
    grad_in = input_sum.astype(jnp.bfloat16)
    grad_mean = product(inputs_wide.T, upstream) / TOKENS
    grad_low = grad_mean.astype(jnp.bfloat16)
    left_rows = []
    right_rows = []
    for block_row in range(D // BLK):
        left_blocks = []
        right_blocks = []
        for block_col in range(E // BLK):
            block = grad_low[block_row * BLK:(block_row + 1) * BLK, block_col * BLK:(block_col + 1) * BLK].astype(jnp.float32)
            left_blocks.append(inverse_root(product(block, block.T)))
            right_blocks.append(inverse_root(product(block.T, block)))
        left_rows.append(jnp.concatenate(left_blocks, axis=1))
        right_rows.append(jnp.concatenate(right_blocks, axis=1))
    return (layer_out, grad_in, jnp.stack(left_rows), jnp.stack(right_rows))
```

```python
import functools

import jax
import jax.numpy as jnp
from jax import lax
from jax.experimental import pallas as pl
from jax.experimental.pallas import tpu as pltpu
from jax.sharding import PartitionSpec as P

ITERS = 6
Y_LO = 4
VMEM = pl.BlockSpec(memory_space=pltpu.VMEM)
SMEM = pl.BlockSpec(memory_space=pltpu.SMEM)
F32 = jnp.float32
BF16 = jnp.bfloat16


def mm(left, right, dims=((1,), (0,))):
    return lax.dot_general(left, right, (dims, ((), ())), preferred_element_type=F32)


def grad_kernel(tokens_all, x_ref, g_ref, grad_ref):
    grad = mm(x_ref[...], g_ref[...], ((0,), (0,)))
    grad_ref[...] = (grad * (1.0 / tokens_all)).astype(BF16)


def sum_kernel(parts_ref, out_ref):
    groups, slab = parts_ref.shape[0] // out_ref.shape[0], out_ref.shape[0]
    total = parts_ref[:slab, :].astype(F32)
    for k in range(1, groups):
        total = total + parts_ref[k * slab : (k + 1) * slab, :].astype(F32)
    out_ref[...] = total.astype(BF16)


def outputs_kernel(place_ref, x_ref, g_ref, w_ref, *rest):
    parts = (len(rest) - 2) // 2
    layer_refs, input_refs, (layer_all, input_all) = rest[:parts], rest[parts : 2 * parts], rest[2 * parts :]
    layer_all[...] = mm(x_ref[...], w_ref[...]).astype(BF16)
    input_all[...] = mm(g_ref[...], w_ref[...], ((1,), (1,))).astype(BF16)
    chunk = x_ref.shape[0] // parts
    for d in range(parts):
        for refs, whole, own in ((layer_refs, layer_all, place_ref[0]), (input_refs, input_all, place_ref[1])):
            start = pl.multiple_of(lax.rem(own + d, parts) * chunk, chunk)
            refs[d][...] = whole[pl.ds(start, chunk), :]


def place_kernel(place_ref, *refs):
    parts = (len(refs) - 2) // 2
    for which in range(2):
        out = refs[2 * parts + which]
        chunk = out.shape[0] // parts
        for d in range(parts):
            start = pl.multiple_of(lax.rem(place_ref[which] + parts - d, parts) * chunk, chunk)
            out[pl.ds(start, chunk), :] = refs[which * parts + d][...]


def newton_kernel(slab, place_ref, *refs):
    groups = len(refs) - 5
    chunk_refs = refs[:groups]
    left_ref, right_ref, block, wide, low = refs[groups:]
    extent = block.shape[0]
    z, y = place_ref[0], place_ref[1]
    for d in range(groups):
        base = lax.rem(z + groups - d, groups) * (Y_LO * slab)
        for e in range(Y_LO):
            start = pl.multiple_of(base + lax.rem(y + Y_LO - e, Y_LO) * slab, slab)
            block[pl.ds(start, slab), :] = chunk_refs[d][e * slab : (e + 1) * slab, :]
    first_row = pl.multiple_of((z * Y_LO + y) * slab, slab)
    row_ids = lax.broadcasted_iota(jnp.int32, (extent, extent), 0)
    column_ids = lax.broadcasted_iota(jnp.int32, (extent, extent), 1)
    own_rows = first_row + lax.broadcasted_iota(jnp.int32, (slab, extent), 0)
    own_columns = lax.broadcasted_iota(jnp.int32, (slab, extent), 1)
    b = block[...]
    rows = []
    for which in range(2):
        stat = mm(b, b, ((1,), (1,))) if which == 0 else mm(b, b, ((0,), (0,)))
        stat = jnp.where(row_ids == column_ids, stat + 1e-06, stat)
        square = jnp.sum(jnp.sum(stat * stat, axis=0, keepdims=True), axis=1, keepdims=True)
        scaling = 0.4 * jnp.sqrt(square + 1e-06)
        quarter = stat * (0.25 / scaling)
        wide[which] = quarter
        low[which] = quarter.astype(BF16)
        start = 1.0 / jnp.sqrt(jnp.sqrt(scaling))
        eye = jnp.where(own_rows == own_columns, 1.25, 0.0)
        rows.append(start * (eye - wide[which, pl.ds(first_row, slab), :]))

    def step(_, rows):
        new = []
        for which in range(2):
            n_low = low[which]
            n_wide = wide[which]
            c = mm(n_low, n_low) - 2.5 * n_wide
            c_low = c.astype(BF16)
            h = (3.125 * c + mm(c_low, c_low)).astype(BF16)
            n_new = 2.44140625 * n_wide + mm(h, n_low)
            wide[which] = n_new
            new_low = n_new.astype(BF16)
            low[which] = new_low
            new.append(1.25 * rows[which] - mm(rows[which].astype(BF16), new_low))
        return tuple(new)

    rows = lax.fori_loop(0, ITERS - 2, step, tuple(rows))
    ends = list(rows)
    for _ in range(4):
        for which in range(2):
            ends[which] = 1.25 * ends[which] - mm(ends[which].astype(BF16), low[which])
    for which, out in ((0, left_ref), (1, right_ref)):
        out[0] = 1.25 * rows[which] - mm(ends[which].astype(BF16), low[which])


def shifted(values, axis, pairs):
    return lax.ppermute(values, axis, pairs)


def exchange_reduce(pieces, axis):
    parts = len(pieces)
    got = [
        shifted(pieces[d], axis, [(i, (i + d) % parts) for i in range(parts)]) for d in range(1, parts)
    ]
    total = pieces[0].astype(F32)
    for piece in got:
        total = total + piece.astype(F32)
    return total.astype(BF16)


def exchange_gather(piece, axis, parts):
    return [piece] + [
        shifted(piece, axis, [(i, (i + d) % parts) for i in range(parts)]) for d in range(1, parts)
    ]


def shards(x_in, grad_out, weight):
    extent = weight.shape[0]
    tokens = x_in.shape[0]
    groups = lax.axis_size("dp")
    slab = extent // groups
    z_size = groups // Y_LO
    tensor, precond = lax.axis_size("tensor"), lax.axis_size("precond")
    parts = tensor
    place = jnp.stack([lax.axis_index("precond"), lax.axis_index("tensor")]).astype(jnp.int32)
    me = lax.axis_index("dp")
    block_place = jnp.stack([lax.div(me, Y_LO), lax.rem(me, Y_LO)]).astype(jnp.int32)

    grad_part = pl.pallas_call(
        functools.partial(grad_kernel, tokens * groups),
        out_shape=jax.ShapeDtypeStruct((extent, extent), BF16),
        in_specs=[VMEM, VMEM],
        out_specs=VMEM,
        compiler_params=pltpu.CompilerParams(vmem_limit_bytes=32 * 2**20),
        cost_estimate=pl.CostEstimate(flops=2 * tokens * extent * extent, bytes_accessed=2**20, transcendentals=0),
        name="grad_part",
    )(x_in, grad_out)
    received = lax.all_to_all(grad_part, "dp", 0, 0, tiled=True)
    mine = pl.pallas_call(
        sum_kernel,
        out_shape=jax.ShapeDtypeStruct((slab, extent), BF16),
        in_specs=[VMEM],
        out_specs=VMEM,
        cost_estimate=pl.CostEstimate(flops=extent * extent, bytes_accessed=2**19, transcendentals=0),
        name="grad_sum",
    )(received)

    piece = jax.ShapeDtypeStruct((tokens // parts, extent), BF16)
    pieces = pl.pallas_call(
        outputs_kernel,
        out_shape=[piece] * (2 * parts),
        in_specs=[SMEM, VMEM, VMEM, VMEM],
        out_specs=[VMEM] * (2 * parts),
        scratch_shapes=[pltpu.VMEM((tokens, extent), BF16)] * 2,
        compiler_params=pltpu.CompilerParams(vmem_limit_bytes=32 * 2**20),
        cost_estimate=pl.CostEstimate(flops=4 * tokens * extent * extent, bytes_accessed=2**21, transcendentals=0),
        name="outputs_part",
    )(place, x_in, grad_out, weight)
    layer_mine = exchange_reduce(pieces[:parts], "precond")
    input_mine = exchange_reduce(pieces[parts:], "tensor")
    outputs_in = exchange_gather(layer_mine, "precond", parts) + exchange_gather(input_mine, "tensor", parts)

    near = [mine]
    for d in range(1, Y_LO):
        pairs = [(z * Y_LO + y, z * Y_LO + (y + d) % Y_LO) for z in range(z_size) for y in range(Y_LO)]
        near.append(shifted(mine, "dp", pairs))
    near = jnp.concatenate(near, axis=0)
    chunks = [near]
    for d in range(1, z_size):
        pairs = [(z * Y_LO + y, ((z + d) % z_size) * Y_LO + y) for z in range(z_size) for y in range(Y_LO)]
        chunks.append(shifted(near, "dp", pairs))

    whole = jax.ShapeDtypeStruct((tokens, extent), BF16)
    layer_out, grad_in = pl.pallas_call(
        place_kernel,
        out_shape=[whole, whole],
        in_specs=[SMEM] + [VMEM] * (2 * parts),
        out_specs=[VMEM, VMEM],
        cost_estimate=pl.CostEstimate(flops=0, bytes_accessed=2**19, transcendentals=0),
        name="place",
    )(place, *outputs_in)

    root = jax.ShapeDtypeStruct((1, slab, extent), F32)
    left_root, right_root = pl.pallas_call(
        functools.partial(newton_kernel, slab),
        out_shape=[root, root],
        in_specs=[SMEM] + [VMEM] * z_size,
        out_specs=[VMEM, VMEM],
        scratch_shapes=[
            pltpu.VMEM((extent, extent), BF16),
            pltpu.VMEM((2, extent, extent), F32),
            pltpu.VMEM((2, extent, extent), BF16),
        ],
        compiler_params=pltpu.CompilerParams(vmem_limit_bytes=48 * 2**20),
        cost_estimate=pl.CostEstimate(flops=60 * extent**3, bytes_accessed=2**20, transcendentals=0),
        name="newton",
    )(block_place, *chunks)
    return layer_out, grad_in, left_root, right_root


def solution(mesh):
    in_specs = (P("dp", "precond"), P("dp", "tensor"), P("precond", "tensor"))
    out_specs = (
        P("dp", "tensor"),
        P("dp", "precond"),
        P("precond", "dp", "tensor"),
        P("precond", "dp", "tensor"),
    )
    return jax.shard_map(shards, mesh=mesh, in_specs=in_specs, out_specs=out_specs, check_vma=False)
```

```python
import functools

import jax
import jax.numpy as jnp
from jax import lax
from jax.experimental import pallas as pl
from jax.experimental.pallas import tpu as pltpu
from jax.sharding import PartitionSpec as P

ITERS = 6
VMEM = pl.BlockSpec(memory_space=pltpu.VMEM)
ANY = pl.BlockSpec(memory_space=pl.ANY)
SMEM = pl.BlockSpec(memory_space=pltpu.SMEM)
F32 = jnp.float32
BF16 = jnp.bfloat16


def mm(left, right, dims=((1,), (0,))):
    return lax.dot_general(left, right, (dims, ((), ())), preferred_element_type=F32)


def fetch(sources, targets, sems):
    copies = [pltpu.make_async_copy(src, dst, sems.at[k]) for k, (src, dst) in enumerate(zip(sources, targets))]
    for copy in copies:
        copy.start()
    for copy in copies:
        copy.wait()


def grad_kernel(tokens_all, x_any, g_any, grad_ref, x_ref, g_ref, sems):
    fetch((x_any, g_any), (x_ref, g_ref), sems)
    grad = mm(x_ref[...], g_ref[...], ((0,), (0,)))
    grad_ref[...] = (grad * (1.0 / tokens_all)).astype(BF16)


def pair_sum(left_ref, right_ref):
    return (left_ref[...].astype(F32) + right_ref[...].astype(F32)).astype(BF16)


def sum_kernel(copies, parts_ref, layer_ref, layer_other, input_ref, input_other, out_ref, layer_sum, input_sum):
    slab = parts_ref.shape[0] // copies
    total = parts_ref[:slab, :].astype(F32)
    for k in range(1, copies):
        total = total + parts_ref[k * slab : (k + 1) * slab, :].astype(F32)
    total = total.astype(BF16)
    for k in range(copies):
        out_ref[k * slab : (k + 1) * slab, :] = total
    layer_sum[...] = pair_sum(layer_ref, layer_other)
    input_sum[...] = pair_sum(input_ref, input_other)


def outputs_kernel(x_any, g_any, w_any, after_any, layer_ref, input_ref, x_ref, g_ref, w_ref, sems):
    fetch((x_any, g_any, w_any), (x_ref, g_ref, w_ref), sems)
    layer_ref[...] = mm(x_ref[...], w_ref[...]).astype(BF16)
    input_ref[...] = mm(g_ref[...], w_ref[...], ((1,), (1,))).astype(BF16)


def newton_kernel(
    slab,
    place_ref,
    block_ref,
    layer_ref,
    layer_other,
    input_ref,
    input_other,
    layer_out,
    input_out,
    left_ref,
    right_ref,
    wide,
    low,
):
    layer_out[...] = pair_sum(layer_ref, layer_other)
    input_out[...] = pair_sum(input_ref, input_other)
    extent = block_ref.shape[0]
    first_row = pl.multiple_of(place_ref[0] * slab, slab)
    row_ids = lax.broadcasted_iota(jnp.int32, (extent, extent), 0)
    column_ids = lax.broadcasted_iota(jnp.int32, (extent, extent), 1)
    own_rows = first_row + lax.broadcasted_iota(jnp.int32, (slab, extent), 0)
    own_columns = lax.broadcasted_iota(jnp.int32, (slab, extent), 1)
    b = block_ref[...]
    rows = []
    for which in range(2):
        stat = mm(b, b, ((1,), (1,))) if which == 0 else mm(b, b, ((0,), (0,)))
        stat = jnp.where(row_ids == column_ids, stat + 1e-06, stat)
        square = jnp.sum(jnp.sum(stat * stat, axis=0, keepdims=True), axis=1, keepdims=True)
        scaling = 0.4 * jnp.sqrt(square + 1e-06)
        quarter = stat * (0.25 / scaling)
        wide[which] = quarter
        low[which] = quarter.astype(BF16)
        start = 1.0 / jnp.sqrt(jnp.sqrt(scaling))
        eye = jnp.where(own_rows == own_columns, 1.25, 0.0)
        rows.append(start * (eye - wide[which, pl.ds(first_row, slab), :]))

    def step(_, rows):
        new = []
        for which in range(2):
            n_low = low[which]
            n_wide = wide[which]
            c = mm(n_low, n_low) - 2.5 * n_wide
            c_low = c.astype(BF16)
            h = (3.125 * c + mm(c_low, c_low)).astype(BF16)
            n_new = 2.44140625 * n_wide + mm(h, n_low)
            wide[which] = n_new
            new_low = n_new.astype(BF16)
            low[which] = new_low
            new.append(1.25 * rows[which] - mm(rows[which].astype(BF16), new_low))
        return tuple(new)

    rows = lax.fori_loop(0, ITERS - 2, step, tuple(rows))
    ends = list(rows)
    for _ in range(4):
        for which in range(2):
            ends[which] = 1.25 * ends[which] - mm(ends[which].astype(BF16), low[which])
    for which, out in ((0, left_ref), (1, right_ref)):
        out[0] = 1.25 * rows[which] - mm(ends[which].astype(BF16), low[which])


def exchange(values, axis):
    return lax.all_to_all(values, axis, 0, 0, tiled=True)


def partner(values, axis, flip):
    return lax.ppermute(values, axis, [(i, i ^ flip) for i in range(4)])


def shards(x_in, grad_out, weight):
    extent = weight.shape[0]
    tokens = x_in.shape[0]
    groups = lax.axis_size("dp")
    slab = extent // groups
    place = lax.axis_index("dp").astype(jnp.int32).reshape(1)
    block = jax.ShapeDtypeStruct((extent, extent), BF16)
    whole = jax.ShapeDtypeStruct((tokens, extent), BF16)
    tokens_vmem = pltpu.VMEM((tokens, extent), BF16)

    grad_part = pl.pallas_call(
        functools.partial(grad_kernel, tokens * groups),
        out_shape=block,
        in_specs=[ANY, ANY],
        out_specs=VMEM,
        scratch_shapes=[tokens_vmem, tokens_vmem, pltpu.SemaphoreType.DMA((2,))],
        compiler_params=pltpu.CompilerParams(vmem_limit_bytes=32 * 2**20),
        cost_estimate=pl.CostEstimate(flops=2 * tokens * extent * extent, bytes_accessed=2**20, transcendentals=0),
        name="grad_part",
    )(x_in, grad_out)
    received = exchange(grad_part, "dp")
    layer_part, input_part = pl.pallas_call(
        outputs_kernel,
        out_shape=[whole, whole],
        in_specs=[ANY, ANY, ANY, ANY],
        out_specs=[VMEM, VMEM],
        scratch_shapes=[
            tokens_vmem,
            tokens_vmem,
            pltpu.VMEM((extent, extent), BF16),
            pltpu.SemaphoreType.DMA((3,)),
        ],
        compiler_params=pltpu.CompilerParams(vmem_limit_bytes=32 * 2**20),
        cost_estimate=pl.CostEstimate(flops=4 * tokens * extent * extent, bytes_accessed=2**20, transcendentals=0),
        name="outputs_part",
    )(x_in, grad_out, weight, grad_part)
    copies, layer_sum, input_sum = pl.pallas_call(
        functools.partial(sum_kernel, groups),
        out_shape=[block, whole, whole],
        in_specs=[VMEM] * 5,
        out_specs=[VMEM] * 3,
        cost_estimate=pl.CostEstimate(flops=extent * extent, bytes_accessed=2**20, transcendentals=0),
        name="sums",
    )(received, layer_part, partner(layer_part, "precond", 1), input_part, partner(input_part, "tensor", 1))
    grad_low = exchange(copies, "dp")

    root = jax.ShapeDtypeStruct((1, slab, extent), F32)
    return pl.pallas_call(
        functools.partial(newton_kernel, slab),
        out_shape=[whole, whole, root, root],
        in_specs=[SMEM] + [VMEM] * 5,
        out_specs=[VMEM] * 4,
        scratch_shapes=[
            pltpu.VMEM((2, extent, extent), F32),
            pltpu.VMEM((2, extent, extent), BF16),
        ],
        compiler_params=pltpu.CompilerParams(vmem_limit_bytes=48 * 2**20),
        cost_estimate=pl.CostEstimate(flops=60 * extent**3, bytes_accessed=2**20, transcendentals=0),
        name="newton",
    )(place, grad_low, layer_sum, partner(layer_sum, "precond", 2), input_sum, partner(input_sum, "tensor", 2))


def solution(mesh):
    in_specs = (P("dp", "precond"), P("dp", "tensor"), P("precond", "tensor"))
    out_specs = (
        P("dp", "tensor"),
        P("dp", "precond"),
        P("precond", "dp", "tensor"),
        P("precond", "dp", "tensor"),
    )
    return jax.shard_map(shards, mesh=mesh, in_specs=in_specs, out_specs=out_specs, check_vma=False)
```

```python
import functools

import jax
import jax.numpy as jnp
from jax import lax
from jax.experimental import pallas as pl
from jax.experimental.pallas import tpu as pltpu
from jax.sharding import PartitionSpec as P

ITERS = 6
VMEM = pl.BlockSpec(memory_space=pltpu.VMEM)
HBM = pl.BlockSpec(memory_space=pltpu.HBM)
ANY = pl.BlockSpec(memory_space=pl.ANY)
SMEM = pl.BlockSpec(memory_space=pltpu.SMEM)
F32 = jnp.float32
BF16 = jnp.bfloat16


def mm(left, right, dims=((1,), (0,))):
    return lax.dot_general(left, right, (dims, ((), ())), preferred_element_type=F32)


def fetch(sources, targets, sems):
    copies = [pltpu.make_async_copy(src, dst, sems.at[k]) for k, (src, dst) in enumerate(zip(sources, targets))]
    for copy in copies:
        copy.start()
    for copy in copies:
        copy.wait()


def grad_kernel(tokens_all, x_any, g_any, grad_ref, x_ref, g_ref, sems):
    fetch((x_any, g_any), (x_ref, g_ref), sems)
    grad = mm(x_ref[...], g_ref[...], ((0,), (0,)))
    grad_ref[...] = (grad * (1.0 / tokens_all)).astype(BF16)


def pair_sum(left_ref, right_ref):
    return (left_ref[...].astype(F32) + right_ref[...].astype(F32)).astype(BF16)


def sum_kernel(copies, parts_ref, layer_ref, layer_other, input_ref, input_other, out_ref, layer_sum, input_sum):
    slab = parts_ref.shape[0] // copies
    total = parts_ref[:slab, :].astype(F32)
    for k in range(1, copies):
        total = total + parts_ref[k * slab : (k + 1) * slab, :].astype(F32)
    total = total.astype(BF16)
    for k in range(copies):
        out_ref[k * slab : (k + 1) * slab, :] = total
    layer_sum[...] = pair_sum(layer_ref, layer_other)
    input_sum[...] = pair_sum(input_ref, input_other)


def outputs_kernel(x_any, g_any, w_any, after_any, layer_ref, input_ref, x_ref, g_ref, w_ref, sems):
    fetch((x_any, g_any, w_any), (x_ref, g_ref, w_ref), sems)
    layer_ref[...] = mm(x_ref[...], w_ref[...]).astype(BF16)
    input_ref[...] = mm(g_ref[...], w_ref[...], ((1,), (1,))).astype(BF16)


def middle_kernel(input_ref, input_other, layer_ref, input_out, layer_copy):
    input_out[...] = pair_sum(input_ref, input_other)
    layer_copy[...] = layer_ref[...]


def last_kernel(layer_ref, layer_other, after_any, layer_out):
    layer_out[...] = pair_sum(layer_ref, layer_other)


def staged(units):
    waiting = None
    for product, use in units:
        result = product()
        if waiting is not None:
            waiting[0](waiting[1])
        waiting = (use, result)
    waiting[0](waiting[1])


def newton_kernel(slab, place_ref, block_ref, left_ref, right_ref, wide, n_low, c_low, h_low, row):
    extent = block_ref.shape[0]
    half = extent // 2
    cuts = (slice(0, half), slice(half, extent))
    sides = ((0, cuts[0]), (0, cuts[1]), (1, cuts[0]), (1, cuts[1]))
    first_row = pl.multiple_of(place_ref[0] * slab, slab)
    outs = (left_ref, right_ref)
    turned = h_low.at[1]
    turned[...] = block_ref[...].T
    on_diagonal = lax.broadcasted_iota(jnp.int32, (half, half), 0) == lax.broadcasted_iota(jnp.int32, (half, half), 1)
    own = first_row + lax.broadcasted_iota(jnp.int32, (slab, extent), 0)
    eye = jnp.where(own == lax.broadcasted_iota(jnp.int32, (slab, extent), 1), 1.25, 0.0)
    squares = [0.0, 0.0]
    quarters = [None, None]

    def gram(side, cut):
        if side == 0:
            return mm(block_ref[...], turned[:, cut])
        return mm(turned[...], block_ref[:, cut])

    def keep_gram(side, cut, product):
        for rows in cuts:
            stat = product[rows]
            if rows == cut:
                stat = jnp.where(on_diagonal, stat + 1e-06, stat)
            wide[side, rows, cut] = stat
            squares[side] = squares[side] + jnp.sum(stat * stat, axis=0, keepdims=True)
        if cut.stop == extent:
            scaling = 0.4 * jnp.sqrt(jnp.sum(squares[side], axis=1, keepdims=True) + 1e-06)
            quarter = 0.25 / scaling
            quarters[side] = quarter
            n_low[side, 0, :extent, :] = (wide[side] * quarter).astype(BF16)
            start = 1.0 / jnp.sqrt(jnp.sqrt(scaling))
            first = start * (eye - quarter * wide[side, pl.ds(first_row, slab), :])
            row[side] = first
            n_low[side, 1, extent:, :] = first.astype(BF16)

    def unit(do, use, side, cut):
        return (lambda: do(side, cut)), (lambda product: use(side, cut, product))

    units = [unit(gram, keep_gram, *at) for at in sides]

    def square_n(now, riders, side, cut):
        return mm(n_low[side, now, : extent + riders, :], n_low[side, now, :extent, cut])

    def keep_c(now, riders, side, cut, product):
        scale = 2.5 * quarters[side] if now == 0 and riders == 0 else 2.5
        c_low[side, :, cut] = (product[:extent] - scale * wide[side, :, cut]).astype(BF16)
        if riders:
            new = 1.25 * row[side, :, cut] - product[extent:]
            row[side, :, cut] = new
            n_low[side, 1 - now, extent:, cut] = new.astype(BF16)

    def square_c(side, cut):
        return mm(c_low[side], c_low[side, :, cut])

    def keep_h(side, cut, product):
        h_low[side, :, cut] = (3.125 * c_low[side, :, cut].astype(F32) + product).astype(BF16)

    def next_n(now, side, cut):
        return mm(h_low[side], n_low[side, now, :extent, cut])

    def keep_n(now, first, side, cut, product):
        scale = 2.44140625 * quarters[side] if first else 2.44140625
        n = scale * wide[side, :, cut] + product
        wide[side, :, cut] = n
        n_low[side, 1 - now, :extent, cut] = n.astype(BF16)

    for k in range(ITERS - 2):
        now, riders = k % 2, (slab if k else 0)
        part = functools.partial
        units += [unit(part(square_n, now, riders), part(keep_c, now, riders), *at) for at in sides]
        units += [unit(square_c, keep_h, *at) for at in sides]
        units += [unit(part(next_n, now), part(keep_n, now, k == 0), *at) for at in sides]
    staged(units)

    now = (ITERS - 2) % 2
    firsts = [1.25 * row[side] - mm(n_low[side, now, extent:, :], n_low[side, now, :extent, :]) for side in range(2)]
    ends = list(firsts)
    for _ in range(4):
        for side in range(2):
            ends[side] = 1.25 * ends[side] - mm(ends[side].astype(BF16), n_low[side, now, :extent, :])
    for side in range(2):
        outs[side][0] = 1.25 * firsts[side] - mm(ends[side].astype(BF16), n_low[side, now, :extent, :])


def limit(mebibytes):
    return pltpu.CompilerParams(vmem_limit_bytes=mebibytes * 2**20)


def exchange(values, axis):
    return lax.all_to_all(values, axis, 0, 0, tiled=True)


def partner(values, axis, flip):
    return lax.ppermute(values, axis, [(i, i ^ flip) for i in range(4)])


def shards(x_in, grad_out, weight):
    extent = weight.shape[0]
    tokens = x_in.shape[0]
    groups = lax.axis_size("dp")
    slab = extent // groups
    place = lax.axis_index("dp").astype(jnp.int32).reshape(1)
    block = jax.ShapeDtypeStruct((extent, extent), BF16)
    whole = jax.ShapeDtypeStruct((tokens, extent), BF16)
    tokens_vmem = pltpu.VMEM((tokens, extent), BF16)

    grad_part = pl.pallas_call(
        functools.partial(grad_kernel, tokens * groups),
        out_shape=block,
        in_specs=[HBM, HBM],
        out_specs=VMEM,
        scratch_shapes=[tokens_vmem, tokens_vmem, pltpu.SemaphoreType.DMA((2,))],
        compiler_params=limit(63),
        cost_estimate=pl.CostEstimate(flops=2 * tokens * extent * extent, bytes_accessed=2**20, transcendentals=0),
        name="grad_part",
    )(x_in, grad_out)
    received = exchange(grad_part, "dp")
    layer_part, input_part = pl.pallas_call(
        outputs_kernel,
        out_shape=[whole, whole],
        in_specs=[HBM, HBM, HBM, ANY],
        out_specs=[VMEM, VMEM],
        scratch_shapes=[
            tokens_vmem,
            tokens_vmem,
            pltpu.VMEM((extent, extent), BF16),
            pltpu.SemaphoreType.DMA((3,)),
        ],
        compiler_params=limit(8),
        cost_estimate=pl.CostEstimate(flops=4 * tokens * extent * extent, bytes_accessed=2**20, transcendentals=0),
        name="outputs_part",
    )(x_in, grad_out, weight, grad_part)
    copies, layer_sum, input_sum = pl.pallas_call(
        functools.partial(sum_kernel, groups),
        out_shape=[block, whole, whole],
        in_specs=[VMEM] * 5,
        out_specs=[VMEM] * 3,
        compiler_params=limit(8),
        cost_estimate=pl.CostEstimate(flops=extent * extent, bytes_accessed=2**20, transcendentals=0),
        name="sums",
    )(received, layer_part, partner(layer_part, "precond", 1), input_part, partner(input_part, "tensor", 1))
    grad_low = exchange(copies, "dp")

    grad_in, layer_copy = pl.pallas_call(
        middle_kernel,
        out_shape=[whole, whole],
        in_specs=[VMEM] * 3,
        out_specs=[VMEM] * 2,
        compiler_params=limit(8),
        cost_estimate=pl.CostEstimate(flops=0, bytes_accessed=2**19, transcendentals=0),
        name="middle",
    )(input_sum, partner(input_sum, "tensor", 2), layer_sum)
    layer_other = partner(layer_copy, "precond", 2)

    root = jax.ShapeDtypeStruct((1, slab, extent), F32)
    left_root, right_root = pl.pallas_call(
        functools.partial(newton_kernel, slab),
        out_shape=[root, root],
        in_specs=[SMEM, VMEM],
        out_specs=[VMEM] * 2,
        scratch_shapes=[
            pltpu.VMEM((2, extent, extent), F32),
            pltpu.VMEM((2, 2, extent + slab, extent), BF16),
            pltpu.VMEM((2, extent, extent), BF16),
            pltpu.VMEM((2, extent, extent), BF16),
            pltpu.VMEM((2, slab, extent), F32),
        ],
        compiler_params=limit(24),
        cost_estimate=pl.CostEstimate(flops=0, bytes_accessed=2**16, transcendentals=0),
        name="newton",
    )(place, grad_low)
    layer_out = pl.pallas_call(
        last_kernel,
        out_shape=whole,
        in_specs=[VMEM, VMEM, ANY],
        out_specs=VMEM,
        compiler_params=limit(8),
        cost_estimate=pl.CostEstimate(flops=0, bytes_accessed=2**18, transcendentals=0),
        name="last",
    )(layer_copy, layer_other, left_root)
    return layer_out, grad_in, left_root, right_root


def solution(mesh):
    in_specs = (P("dp", "precond"), P("dp", "tensor"), P("precond", "tensor"))
    out_specs = (
        P("dp", "tensor"),
        P("dp", "precond"),
        P("precond", "dp", "tensor"),
        P("precond", "dp", "tensor"),
    )
    return jax.shard_map(shards, mesh=mesh, in_specs=in_specs, out_specs=out_specs, check_vma=False)
```

```python
import functools

import jax
import jax.numpy as jnp
from jax import lax
from jax.experimental import pallas as pl
from jax.experimental.pallas import tpu as pltpu
from jax.sharding import PartitionSpec as P

ITERS = 6
CHUNKS = 2
VMEM = pl.BlockSpec(memory_space=pltpu.VMEM)
HBM = pl.BlockSpec(memory_space=pltpu.HBM)
ANY = pl.BlockSpec(memory_space=pl.ANY)
SMEM = pl.BlockSpec(memory_space=pltpu.SMEM)
F32 = jnp.float32
BF16 = jnp.bfloat16


def mm(left, right, dims=((1,), (0,))):
    return lax.dot_general(left, right, (dims, ((), ())), preferred_element_type=F32)


def fetch(sources, targets, sems):
    copies = [pltpu.make_async_copy(src, dst, sems.at[k]) for k, (src, dst) in enumerate(zip(sources, targets))]
    for copy in copies:
        copy.start()
    for copy in copies:
        copy.wait()


def grad_kernel(tokens_all, x_any, g_any, grad_any, x_ref, g_ref, grad_ref, sems, out_sems):
    fetch((x_any, g_any), (x_ref, g_ref), sems)
    copies = []
    chunk = grad_ref.shape[0] // CHUNKS
    for k in range(CHUNKS):
        rows = slice(k * chunk, (k + 1) * chunk)
        grad = mm(x_ref[:, rows], g_ref[...], ((0,), (0,)))
        grad_ref[rows, :] = (grad * (1.0 / tokens_all)).astype(BF16)
        copies.append(pltpu.make_async_copy(grad_ref.at[rows, :], grad_any.at[rows, :], out_sems.at[k]))
        copies[k].start()
    for copy in copies:
        copy.wait()


def pair_sum(left_ref, right_ref):
    return (left_ref[...].astype(F32) + right_ref[...].astype(F32)).astype(BF16)


def sum_kernel(copies, parts_ref, input_ref, input_other, layer_any, out_ref, input_sum):
    slab = parts_ref.shape[0] // copies
    total = parts_ref[:slab, :].astype(F32)
    for k in range(1, copies):
        total = total + parts_ref[k * slab : (k + 1) * slab, :].astype(F32)
    total = total.astype(BF16)
    for k in range(copies):
        out_ref[k * slab : (k + 1) * slab, :] = total
    input_sum[...] = pair_sum(input_ref, input_other)


def outputs_kernel(x_any, g_any, w_any, after_any, layer_ref, input_ref, x_ref, g_ref, w_ref, sems):
    fetch((x_any, g_any, w_any), (x_ref, g_ref, w_ref), sems)
    layer_ref[...] = mm(x_ref[...], w_ref[...]).astype(BF16)
    input_ref[...] = mm(g_ref[...], w_ref[...], ((1,), (1,))).astype(BF16)


def middle_kernel(input_ref, input_other, layer_ref, layer_other, input_out, layer_sum):
    layer_sum[...] = pair_sum(layer_ref, layer_other)
    input_out[...] = pair_sum(input_ref, input_other)


def last_kernel(layer_ref, layer_other, done_ref, layer_out):
    layer_out[...] = pair_sum(layer_ref, layer_other)


def staged(units):
    waiting = None
    for product, use in units:
        result = product()
        if waiting is not None:
            waiting[0](waiting[1])
        waiting = (use, result)
    waiting[0](waiting[1])


def newton_kernel(slab, place_ref, block_ref, left_ref, right_ref, done_ref, wide, n_low, c_low, h_low, row):
    extent = block_ref.shape[0]
    half = extent // 2
    top, low = slice(0, half), slice(half, extent)
    sides = ((0, top), (0, low), (1, top), (1, low))
    first_row = pl.multiple_of(place_ref[0] * slab, slab)
    outs = (left_ref, right_ref)
    turned = h_low.at[1]
    turned[...] = block_ref[...].T
    on_diagonal = lax.broadcasted_iota(jnp.int32, (half, half), 0) == lax.broadcasted_iota(jnp.int32, (half, half), 1)
    own = first_row + lax.broadcasted_iota(jnp.int32, (slab, extent), 0)
    eye = jnp.where(own == lax.broadcasted_iota(jnp.int32, (slab, extent), 1), 1.25, 0.0)
    squares = [None, None]
    quarters = [None, None]

    def keep(ref, cut, values):
        values = values.astype(BF16)
        ref[cut.start : extent, cut] = values
        if cut == top:
            ref[top, low] = values[half:].T

    def gram(side, cut):
        left, right = (block_ref, turned) if side == 0 else (turned, block_ref)
        return mm(left[cut.start :, :], right[:, cut])

    def keep_gram(side, cut, product):
        corner = jnp.where(on_diagonal, product[:half] + 1e-06, product[:half])
        wide[side, cut, cut] = corner
        square = jnp.sum(corner * corner, axis=0, keepdims=True)
        if cut == top:
            below = product[half:]
            wide[side, low, top] = below
            wide[side, top, low] = below.T
            squares[side] = square + 2.0 * jnp.sum(below * below, axis=0, keepdims=True)
            return
        total = jnp.sum(squares[side] + square, axis=1, keepdims=True)
        scaling = 0.4 * jnp.sqrt(total + 1e-06)
        quarter = 0.25 / scaling
        quarters[side] = quarter
        n_low[side, 0, :extent, :] = (wide[side] * quarter).astype(BF16)
        start = 1.0 / jnp.sqrt(jnp.sqrt(scaling))
        first = start * (eye - quarter * wide[side, pl.ds(first_row, slab), :])
        row[side] = first
        n_low[side, 1, extent:, :] = first.astype(BF16)

    def unit(do, use, side, cut):
        return (lambda: do(side, cut)), (lambda product: use(side, cut, product))

    units = [unit(gram, keep_gram, *at) for at in sides]

    def square_n(now, riders, side, cut):
        return mm(n_low[side, now, cut.start : extent + riders, :], n_low[side, now, :extent, cut])

    def keep_c(now, riders, side, cut, product):
        scale = 2.5 * quarters[side] if now == 0 and riders == 0 else 2.5
        size = extent - cut.start
        keep(c_low.at[side], cut, product[:size] - scale * wide[side, cut.start :, cut])
        if riders:
            new = 1.25 * row[side, :, cut] - product[size:]
            row[side, :, cut] = new
            n_low[side, 1 - now, extent:, cut] = new.astype(BF16)

    def square_c(side, cut):
        return mm(c_low[side, cut.start :, :], c_low[side, :, cut])

    def keep_h(side, cut, product):
        keep(h_low.at[side], cut, 3.125 * c_low[side, cut.start :, cut].astype(F32) + product)

    def next_n(now, side, cut):
        return mm(h_low[side, cut.start :, :], n_low[side, now, :extent, cut])

    def keep_n(now, first, side, cut, product):
        scale = 2.44140625 * quarters[side] if first else 2.44140625
        n = scale * wide[side, cut.start :, cut] + product
        wide[side, cut.start :, cut] = n
        keep(n_low.at[side, 1 - now], cut, n)

    for k in range(ITERS - 2):
        now, riders = k % 2, (slab if k else 0)
        part = functools.partial
        units += [unit(part(square_n, now, riders), part(keep_c, now, riders), *at) for at in sides]
        units += [unit(square_c, keep_h, *at) for at in sides]
        units += [unit(part(next_n, now), part(keep_n, now, k == 0), *at) for at in sides]
    staged(units)

    now = (ITERS - 2) % 2
    firsts = [1.25 * row[side] - mm(n_low[side, now, extent:, :], n_low[side, now, :extent, :]) for side in range(2)]
    ends = list(firsts)
    for _ in range(4):
        for side in range(2):
            ends[side] = 1.25 * ends[side] - mm(ends[side].astype(BF16), n_low[side, now, :extent, :])
    for side in range(2):
        outs[side][0] = 1.25 * firsts[side] - mm(ends[side].astype(BF16), n_low[side, now, :extent, :])
    done_ref[...] = jnp.zeros_like(done_ref)


def limit(mebibytes):
    return pltpu.CompilerParams(vmem_limit_bytes=mebibytes * 2**20)


def exchange(values, axis):
    return lax.all_to_all(values, axis, 0, 0, tiled=True)


def partner(values, axis, flip):
    return lax.ppermute(values, axis, [(i, i ^ flip) for i in range(4)])


def shards(x_in, grad_out, weight):
    extent = weight.shape[0]
    tokens = x_in.shape[0]
    groups = lax.axis_size("dp")
    slab = extent // groups
    place = lax.axis_index("dp").astype(jnp.int32).reshape(1)
    block = jax.ShapeDtypeStruct((extent, extent), BF16)
    whole = jax.ShapeDtypeStruct((tokens, extent), BF16)
    tokens_vmem = pltpu.VMEM((tokens, extent), BF16)

    grad_part = pl.pallas_call(
        functools.partial(grad_kernel, tokens * groups),
        out_shape=block,
        in_specs=[HBM, HBM],
        out_specs=HBM,
        scratch_shapes=[
            tokens_vmem,
            tokens_vmem,
            pltpu.VMEM((extent, extent), BF16),
            pltpu.SemaphoreType.DMA((2,)),
            pltpu.SemaphoreType.DMA((CHUNKS,)),
        ],
        compiler_params=limit(63),
        cost_estimate=pl.CostEstimate(flops=2 * tokens * extent * extent, bytes_accessed=2**20, transcendentals=0),
        name="grad_part",
    )(x_in, grad_out)
    received = exchange(grad_part, "dp")
    layer_part, input_part = pl.pallas_call(
        outputs_kernel,
        out_shape=[whole, whole],
        in_specs=[HBM, HBM, HBM, ANY],
        out_specs=[VMEM, VMEM],
        scratch_shapes=[
            tokens_vmem,
            tokens_vmem,
            pltpu.VMEM((extent, extent), BF16),
            pltpu.SemaphoreType.DMA((3,)),
        ],
        compiler_params=limit(8),
        cost_estimate=pl.CostEstimate(flops=4 * tokens * extent * extent, bytes_accessed=2**20, transcendentals=0),
        name="outputs_part",
    )(x_in, grad_out, weight, grad_part)
    layer_near = partner(layer_part, "precond", 1)
    copies, input_sum = pl.pallas_call(
        functools.partial(sum_kernel, groups),
        out_shape=[block, whole],
        in_specs=[VMEM, VMEM, VMEM, ANY],
        out_specs=[VMEM] * 2,
        compiler_params=limit(8),
        cost_estimate=pl.CostEstimate(flops=extent * extent, bytes_accessed=2**20, transcendentals=0),
        name="sums",
    )(received, input_part, partner(input_part, "tensor", 1), layer_near)
    grad_low = exchange(copies, "dp")

    grad_in, layer_sum = pl.pallas_call(
        middle_kernel,
        out_shape=[whole, whole],
        in_specs=[VMEM] * 4,
        out_specs=[VMEM] * 2,
        compiler_params=limit(8),
        cost_estimate=pl.CostEstimate(flops=0, bytes_accessed=2**19, transcendentals=0),
        name="middle",
    )(input_sum, partner(input_sum, "tensor", 2), layer_part, layer_near)
    layer_other = partner(layer_sum, "precond", 2)

    root = jax.ShapeDtypeStruct((1, slab, extent), F32)
    left_root, right_root, done = pl.pallas_call(
        functools.partial(newton_kernel, slab),
        out_shape=[root, root, jax.ShapeDtypeStruct((8, 128), F32)],
        in_specs=[SMEM, VMEM],
        out_specs=[VMEM] * 3,
        scratch_shapes=[
            pltpu.VMEM((2, extent, extent), F32),
            pltpu.VMEM((2, 2, extent + slab, extent), BF16),
            pltpu.VMEM((2, extent, extent), BF16),
            pltpu.VMEM((2, extent, extent), BF16),
            pltpu.VMEM((2, slab, extent), F32),
        ],
        compiler_params=limit(24),
        cost_estimate=pl.CostEstimate(flops=0, bytes_accessed=2**16, transcendentals=0),
        name="newton",
    )(place, grad_low)
    layer_out = pl.pallas_call(
        last_kernel,
        out_shape=whole,
        in_specs=[VMEM, VMEM, VMEM],
        out_specs=VMEM,
        compiler_params=limit(8),
        cost_estimate=pl.CostEstimate(flops=0, bytes_accessed=2**18, transcendentals=0),
        name="last",
    )(layer_sum, layer_other, done)
    return layer_out, grad_in, left_root, right_root


def solution(mesh):
    in_specs = (P("dp", "precond"), P("dp", "tensor"), P("precond", "tensor"))
    out_specs = (
        P("dp", "tensor"),
        P("dp", "precond"),
        P("precond", "dp", "tensor"),
        P("precond", "dp", "tensor"),
    )
    return jax.shard_map(shards, mesh=mesh, in_specs=in_specs, out_specs=out_specs, check_vma=False)
```

```python
import functools

import jax
import jax.numpy as jnp
from jax import lax
from jax.experimental import pallas as pl
from jax.experimental.pallas import tpu as pltpu
from jax.sharding import PartitionSpec as P

ITERS = 6
VMEM = pl.BlockSpec(memory_space=pltpu.VMEM)
HBM = pl.BlockSpec(memory_space=pltpu.HBM)
ANY = pl.BlockSpec(memory_space=pl.ANY)
SMEM = pl.BlockSpec(memory_space=pltpu.SMEM)
F32 = jnp.float32
BF16 = jnp.bfloat16


def mm(left, right, dims=((1,), (0,))):
    return lax.dot_general(left, right, (dims, ((), ())), preferred_element_type=F32)


def fetch(sources, targets, sems):
    copies = [pltpu.make_async_copy(src, dst, sems.at[k]) for k, (src, dst) in enumerate(zip(sources, targets))]
    for copy in copies:
        copy.start()
    for copy in copies:
        copy.wait()


def grad_kernel(tokens_all, x_any, g_any, grad_ref, x_ref, g_ref, sems):
    fetch((x_any, g_any), (x_ref, g_ref), sems)
    grad = mm(x_ref[...], g_ref[...], ((0,), (0,)))
    grad_ref[...] = (grad * (1.0 / tokens_all)).astype(BF16)


def pair_sum(left_ref, right_ref):
    return (left_ref[...].astype(F32) + right_ref[...].astype(F32)).astype(BF16)


def sum_kernel(copies, parts_ref, input_ref, input_other, layer_any, out_ref, input_sum):
    slab = parts_ref.shape[0] // copies
    total = parts_ref[:slab, :].astype(F32)
    for k in range(1, copies):
        total = total + parts_ref[k * slab : (k + 1) * slab, :].astype(F32)
    total = total.astype(BF16)
    for k in range(copies):
        out_ref[k * slab : (k + 1) * slab, :] = total
    input_sum[...] = pair_sum(input_ref, input_other)


def outputs_kernel(x_any, g_any, w_any, after_any, layer_ref, input_ref, x_ref, g_ref, w_ref, sems):
    fetch((x_any, g_any, w_any), (x_ref, g_ref, w_ref), sems)
    layer_ref[...] = mm(x_ref[...], w_ref[...]).astype(BF16)
    input_ref[...] = mm(g_ref[...], w_ref[...], ((1,), (1,))).astype(BF16)


def middle_kernel(input_ref, input_other, layer_ref, layer_other, input_out, layer_sum):
    layer_sum[...] = pair_sum(layer_ref, layer_other)
    input_out[...] = pair_sum(input_ref, input_other)


def last_kernel(layer_ref, layer_other, left_ref, right_ref, layer_out, left_out, right_out):
    layer_out[...] = pair_sum(layer_ref, layer_other)
    left_out[...] = left_ref[...]
    right_out[...] = right_ref[...]


def staged(units):
    waiting = None
    for product, use in units:
        result = product()
        if waiting is not None:
            waiting[0](waiting[1])
        waiting = (use, result)
    waiting[0](waiting[1])


def newton_kernel(slab, place_ref, block_ref, left_ref, right_ref, wide, n_low, c_low, h_low, row):
    extent = block_ref.shape[0]
    half = extent // 2
    top, low = slice(0, half), slice(half, extent)
    sides = ((0, top), (0, low), (1, top), (1, low))
    first_row = pl.multiple_of(place_ref[0] * slab, slab)
    outs = (left_ref, right_ref)
    turned = h_low.at[1]
    turned[...] = block_ref[...].T
    on_diagonal = lax.broadcasted_iota(jnp.int32, (half, half), 0) == lax.broadcasted_iota(jnp.int32, (half, half), 1)
    own = first_row + lax.broadcasted_iota(jnp.int32, (slab, extent), 0)
    eye = jnp.where(own == lax.broadcasted_iota(jnp.int32, (slab, extent), 1), 1.25, 0.0)
    squares = [None, None]
    quarters = [None, None]

    def keep(ref, cut, values):
        values = values.astype(BF16)
        ref[cut.start : extent, cut] = values
        if cut == top:
            ref[top, low] = values[half:].T

    def gram(side, cut):
        left, right = (block_ref, turned) if side == 0 else (turned, block_ref)
        return mm(left[cut.start :, :], right[:, cut])

    def keep_gram(side, cut, product):
        corner = jnp.where(on_diagonal, product[:half] + 1e-06, product[:half])
        wide[side, cut, cut] = corner
        square = jnp.sum(corner * corner, axis=0, keepdims=True)
        if cut == top:
            below = product[half:]
            wide[side, low, top] = below
            wide[side, top, low] = below.T
            squares[side] = square + 2.0 * jnp.sum(below * below, axis=0, keepdims=True)
            return
        total = jnp.sum(squares[side] + square, axis=1, keepdims=True)
        scaling = 0.4 * jnp.sqrt(total + 1e-06)
        quarter = 0.25 / scaling
        quarters[side] = quarter
        n_low[side, 0, :extent, :] = (wide[side] * quarter).astype(BF16)
        start = 1.0 / jnp.sqrt(jnp.sqrt(scaling))
        first = start * (eye - quarter * wide[side, pl.ds(first_row, slab), :])
        row[side] = first
        n_low[side, 1, extent:, :] = first.astype(BF16)

    def unit(do, use, side, cut):
        return (lambda: do(side, cut)), (lambda product: use(side, cut, product))

    units = [unit(gram, keep_gram, *at) for at in sides]

    def square_n(now, riders, side, cut):
        return mm(n_low[side, now, cut.start : extent + riders, :], n_low[side, now, :extent, cut])

    def keep_c(now, riders, side, cut, product):
        scale = 2.5 * quarters[side] if now == 0 and riders == 0 else 2.5
        size = extent - cut.start
        keep(c_low.at[side], cut, product[:size] - scale * wide[side, cut.start :, cut])
        if riders:
            new = 1.25 * row[side, :, cut] - product[size:]
            row[side, :, cut] = new
            n_low[side, 1 - now, extent:, cut] = new.astype(BF16)

    def square_c(side, cut):
        return mm(c_low[side, cut.start :, :], c_low[side, :, cut])

    def keep_h(side, cut, product):
        keep(h_low.at[side], cut, 3.125 * c_low[side, cut.start :, cut].astype(F32) + product)

    def next_n(now, side, cut):
        return mm(h_low[side, cut.start :, :], n_low[side, now, :extent, cut])

    def keep_n(now, first, side, cut, product):
        scale = 2.44140625 * quarters[side] if first else 2.44140625
        n = scale * wide[side, cut.start :, cut] + product
        wide[side, cut.start :, cut] = n
        keep(n_low.at[side, 1 - now], cut, n)

    for k in range(ITERS - 2):
        now, riders = k % 2, (slab if k else 0)
        part = functools.partial
        units += [unit(part(square_n, now, riders), part(keep_c, now, riders), *at) for at in sides]
        units += [unit(square_c, keep_h, *at) for at in sides]
        units += [unit(part(next_n, now), part(keep_n, now, k == 0), *at) for at in sides]
    now = (ITERS - 2) % 2
    units += [unit(functools.partial(square_n, now, slab), functools.partial(keep_c, now, slab), *at) for at in sides]
    staged(units)

    ends = [row[side] for side in range(2)]
    for _ in range(2):
        for side in range(2):
            ends[side] = 1.5625 * ends[side] + mm(ends[side].astype(BF16), c_low[side])
    for side in range(2):
        outs[side][0] = 1.25 * row[side] - mm(ends[side].astype(BF16), n_low[side, now, :extent, :])


def in_hbm(values):
    return pltpu.with_memory_space_constraint(values, pltpu.HBM)


def limit(mebibytes):
    return pltpu.CompilerParams(vmem_limit_bytes=mebibytes * 2**20)


def exchange(values, axis):
    return lax.all_to_all(values, axis, 0, 0, tiled=True)


def partner(values, axis, flip):
    return lax.ppermute(values, axis, [(i, i ^ flip) for i in range(4)])


def shards(x_in, grad_out, weight):
    extent = weight.shape[0]
    tokens = x_in.shape[0]
    groups = lax.axis_size("dp")
    slab = extent // groups
    place = lax.axis_index("dp").astype(jnp.int32).reshape(1)
    block = pltpu.VMEM((extent, extent), BF16)
    whole = jax.ShapeDtypeStruct((tokens, extent), BF16)
    tokens_vmem = pltpu.VMEM((tokens, extent), BF16)

    grad_part = pl.pallas_call(
        functools.partial(grad_kernel, tokens * groups),
        out_shape=block,
        in_specs=[HBM, HBM],
        out_specs=VMEM,
        scratch_shapes=[tokens_vmem, tokens_vmem, pltpu.SemaphoreType.DMA((2,))],
        compiler_params=limit(8),
        cost_estimate=pl.CostEstimate(flops=2 * tokens * extent * extent, bytes_accessed=2**20, transcendentals=0),
        name="grad_part",
    )(in_hbm(x_in), in_hbm(grad_out))
    received = exchange(grad_part, "dp")
    layer_part, input_part = pl.pallas_call(
        outputs_kernel,
        out_shape=[whole, whole],
        in_specs=[HBM, HBM, HBM, ANY],
        out_specs=[VMEM, VMEM],
        scratch_shapes=[
            tokens_vmem,
            tokens_vmem,
            pltpu.VMEM((extent, extent), BF16),
            pltpu.SemaphoreType.DMA((3,)),
        ],
        compiler_params=limit(8),
        cost_estimate=pl.CostEstimate(flops=4 * tokens * extent * extent, bytes_accessed=2**20, transcendentals=0),
        name="outputs_part",
    )(x_in, grad_out, weight, grad_part)
    layer_near = partner(layer_part, "precond", 1)
    copies, input_sum = pl.pallas_call(
        functools.partial(sum_kernel, groups),
        out_shape=[block, whole],
        in_specs=[VMEM, VMEM, VMEM, ANY],
        out_specs=[VMEM] * 2,
        compiler_params=limit(8),
        cost_estimate=pl.CostEstimate(flops=extent * extent, bytes_accessed=2**20, transcendentals=0),
        name="sums",
    )(received, input_part, partner(input_part, "tensor", 1), layer_near)
    grad_low = exchange(copies, "dp")

    grad_in, layer_sum = pl.pallas_call(
        middle_kernel,
        out_shape=[whole, whole],
        in_specs=[VMEM] * 4,
        out_specs=[VMEM] * 2,
        compiler_params=limit(8),
        cost_estimate=pl.CostEstimate(flops=0, bytes_accessed=2**19, transcendentals=0),
        name="middle",
    )(input_sum, partner(input_sum, "tensor", 2), layer_part, layer_near)
    layer_other = partner(layer_sum, "precond", 2)

    root = jax.ShapeDtypeStruct((1, slab, extent), F32)
    left_near, right_near = pl.pallas_call(
        functools.partial(newton_kernel, slab),
        out_shape=[pltpu.VMEM((1, slab, extent), F32)] * 2,
        in_specs=[SMEM, VMEM],
        out_specs=[VMEM] * 2,
        scratch_shapes=[
            pltpu.VMEM((2, extent, extent), F32),
            pltpu.VMEM((2, 2, extent + slab, extent), BF16),
            pltpu.VMEM((2, extent, extent), BF16),
            pltpu.VMEM((2, extent, extent), BF16),
            pltpu.VMEM((2, slab, extent), F32),
        ],
        compiler_params=limit(24),
        cost_estimate=pl.CostEstimate(flops=0, bytes_accessed=2**16, transcendentals=0),
        name="newton",
    )(place, grad_low)
    layer_out, left_root, right_root = pl.pallas_call(
        last_kernel,
        out_shape=[whole, root, root],
        in_specs=[VMEM] * 4,
        out_specs=[VMEM] * 3,
        compiler_params=limit(8),
        cost_estimate=pl.CostEstimate(flops=0, bytes_accessed=2**18, transcendentals=0),
        name="last",
    )(layer_sum, layer_other, left_near, right_near)
    return layer_out, grad_in, left_root, right_root


def solution(mesh):
    in_specs = (P("dp", "precond"), P("dp", "tensor"), P("precond", "tensor"))
    out_specs = (
        P("dp", "tensor"),
        P("dp", "precond"),
        P("precond", "dp", "tensor"),
        P("precond", "dp", "tensor"),
    )
    return jax.shard_map(shards, mesh=mesh, in_specs=in_specs, out_specs=out_specs, check_vma=False)
```

```python
import functools

import jax
import jax.numpy as jnp
from jax import lax
from jax.experimental import pallas as pl
from jax.experimental.pallas import tpu as pltpu
from jax.sharding import PartitionSpec as P

ITERS = 6
CHUNKS = 4
Y_LO = 4
VMEM = pl.BlockSpec(memory_space=pltpu.VMEM)
HBM = pl.BlockSpec(memory_space=pltpu.HBM)
ANY = pl.BlockSpec(memory_space=pl.ANY)
SMEM = pl.BlockSpec(memory_space=pltpu.SMEM)
F32 = jnp.float32
BF16 = jnp.bfloat16


def mm(left, right, dims=((1,), (0,))):
    return lax.dot_general(left, right, (dims, ((), ())), preferred_element_type=F32)


def fetch(sources, targets, sems):
    copies = []
    for source, target in zip(sources, targets):
        size = source.shape[0] // CHUNKS
        for k in range(CHUNKS):
            rows = slice(k * size, (k + 1) * size)
            copies.append(pltpu.make_async_copy(source.at[rows, :], target.at[rows, :], sems.at[len(copies)]))
    for copy in copies:
        copy.start()
    for copy in copies:
        copy.wait()


def grad_kernel(tokens_all, x_any, g_any, grad_ref, x_ref, g_ref, sems):
    fetch((x_any, g_any), (x_ref, g_ref), sems)
    grad = mm(x_ref[...], g_ref[...], ((0,), (0,)))
    grad_ref[...] = (grad * (1.0 / tokens_all)).astype(BF16)


def pair_sum(left_ref, right_ref):
    return (left_ref[...].astype(F32) + right_ref[...].astype(F32)).astype(BF16)


def sum_kernel(copies, parts_ref, input_ref, input_other, layer_any, out_ref, input_sum):
    slab = parts_ref.shape[0] // copies
    total = parts_ref[:slab, :].astype(F32)
    for k in range(1, copies):
        total = total + parts_ref[k * slab : (k + 1) * slab, :].astype(F32)
    out_ref[...] = total.astype(BF16)
    input_sum[...] = pair_sum(input_ref, input_other)


def copies_kernel(half_ref, other_ref, out_ref):
    slab = half_ref.shape[0]
    total = pair_sum(half_ref, other_ref)
    for k in range(out_ref.shape[0] // slab):
        out_ref[k * slab : (k + 1) * slab, :] = total


def outputs_kernel(x_any, g_any, w_any, after_any, layer_ref, input_ref, x_ref, g_ref, w_ref, sems):
    fetch((x_any, g_any, w_any), (x_ref, g_ref, w_ref), sems)
    layer_ref[...] = mm(x_ref[...], w_ref[...]).astype(BF16)
    input_ref[...] = mm(g_ref[...], w_ref[...], ((1,), (1,))).astype(BF16)


def middle_kernel(input_ref, input_other, layer_ref, layer_other, input_out, layer_sum):
    layer_sum[...] = pair_sum(layer_ref, layer_other)
    input_out[...] = pair_sum(input_ref, input_other)


def last_kernel(layer_ref, layer_other, left_ref, right_ref, layer_out, left_out, right_out):
    layer_out[...] = pair_sum(layer_ref, layer_other)
    left_out[...] = left_ref[...]
    right_out[...] = right_ref[...]


def staged(units):
    waiting = None
    for product, use in units:
        result = product()
        if waiting is not None:
            waiting[0](waiting[1])
        waiting = (use, result)
    waiting[0](waiting[1])


def newton_kernel(slab, place_ref, block_ref, left_ref, right_ref, wide, n_low, c_low, h_low, row):
    extent = block_ref.shape[0]
    half = extent // 2
    top, low = slice(0, half), slice(half, extent)
    sides = ((0, top), (0, low), (1, top), (1, low))
    first_row = pl.multiple_of(place_ref[0] * slab, slab)
    outs = (left_ref, right_ref)
    turned = h_low.at[1]
    turned[...] = block_ref[...].T
    on_diagonal = lax.broadcasted_iota(jnp.int32, (half, half), 0) == lax.broadcasted_iota(jnp.int32, (half, half), 1)
    own = first_row + lax.broadcasted_iota(jnp.int32, (slab, extent), 0)
    eye = jnp.where(own == lax.broadcasted_iota(jnp.int32, (slab, extent), 1), 1.25, 0.0)
    squares = [None, None]
    quarters = [None, None]

    def keep(ref, cut, values):
        values = values.astype(BF16)
        ref[cut.start : extent, cut] = values
        if cut == top:
            ref[top, low] = values[half:].T

    def gram(side, cut):
        if side == 0:
            return mm(block_ref[cut.start :, :], block_ref[cut, :], ((1,), (1,)))
        return mm(turned[cut.start :, :], block_ref[:, cut])

    def keep_gram(side, cut, product):
        corner = jnp.where(on_diagonal, product[:half] + 1e-06, product[:half])
        wide[side, cut, cut] = corner
        square = jnp.sum(corner * corner, axis=0, keepdims=True)
        if cut == top:
            below = product[half:]
            wide[side, low, top] = below
            wide[side, top, low] = below.T
            squares[side] = square + 2.0 * jnp.sum(below * below, axis=0, keepdims=True)
            return
        total = jnp.sum(squares[side] + square, axis=1, keepdims=True)
        scaling = 0.4 * jnp.sqrt(total + 1e-06)
        quarter = 0.25 / scaling
        quarters[side] = quarter
        n_low[side, 0, :extent, :] = (wide[side] * quarter).astype(BF16)
        start = 1.0 / jnp.sqrt(jnp.sqrt(scaling))
        first = start * (eye - quarter * wide[side, pl.ds(first_row, slab), :])
        row[side] = first
        n_low[side, 1, extent:, :] = first.astype(BF16)

    def unit(do, use, side, cut):
        return (lambda: do(side, cut)), (lambda product: use(side, cut, product))

    units = [unit(gram, keep_gram, *at) for at in sides]

    def square_n(now, riders, side, cut):
        return mm(n_low[side, now, cut.start : extent + riders, :], n_low[side, now, :extent, cut])

    def keep_c(now, riders, side, cut, product):
        scale = 2.5 * quarters[side] if now == 0 and riders == 0 else 2.5
        size = extent - cut.start
        keep(c_low.at[side], cut, product[:size] - scale * wide[side, cut.start :, cut])
        if riders:
            new = 1.25 * row[side, :, cut] - product[size:]
            row[side, :, cut] = new
            n_low[side, 1 - now, extent:, cut] = new.astype(BF16)

    def square_c(side, cut):
        return mm(c_low[side, cut.start :, :], c_low[side, :, cut])

    def keep_h(side, cut, product):
        keep(h_low.at[side], cut, 3.125 * c_low[side, cut.start :, cut].astype(F32) + product)

    def next_n(now, side, cut):
        return mm(h_low[side, cut.start :, :], n_low[side, now, :extent, cut])

    def keep_n(now, first, side, cut, product):
        scale = 2.44140625 * quarters[side] if first else 2.44140625
        n = scale * wide[side, cut.start :, cut] + product
        wide[side, cut.start :, cut] = n
        keep(n_low.at[side, 1 - now], cut, n)

    for k in range(ITERS - 2):
        now, riders = k % 2, (slab if k else 0)
        part = functools.partial
        units += [unit(part(square_n, now, riders), part(keep_c, now, riders), *at) for at in sides]
        units += [unit(square_c, keep_h, *at) for at in sides]
        units += [unit(part(next_n, now), part(keep_n, now, k == 0), *at) for at in sides]
    now = (ITERS - 2) % 2
    units += [unit(functools.partial(square_n, now, slab), functools.partial(keep_c, now, slab), *at) for at in sides]
    staged(units)

    ends = [row[side] for side in range(2)]
    for _ in range(2):
        for side in range(2):
            ends[side] = 1.5625 * ends[side] + mm(ends[side].astype(BF16), c_low[side])
    for side in range(2):
        outs[side][0] = 1.25 * row[side] - mm(ends[side].astype(BF16), n_low[side, now, :extent, :])


def in_hbm(values):
    return pltpu.with_memory_space_constraint(values, pltpu.HBM)


def limit(mebibytes):
    return pltpu.CompilerParams(vmem_limit_bytes=mebibytes * 2**20)


def exchange(values, groups):
    return lax.all_to_all(values, "dp", 0, 0, tiled=True, axis_index_groups=groups)


def partner(values, axis, flip):
    return lax.ppermute(values, axis, [(i, i ^ flip) for i in range(4)])


def shards(x_in, grad_out, weight):
    extent = weight.shape[0]
    tokens = x_in.shape[0]
    groups = lax.axis_size("dp")
    slab = extent // groups
    place = lax.axis_index("dp").astype(jnp.int32).reshape(1)
    block = pltpu.VMEM((extent, extent), BF16)
    whole = jax.ShapeDtypeStruct((tokens, extent), BF16)
    tokens_vmem = pltpu.VMEM((tokens, extent), BF16)

    grad_part = pl.pallas_call(
        functools.partial(grad_kernel, tokens * groups),
        out_shape=block,
        in_specs=[HBM, HBM],
        out_specs=VMEM,
        scratch_shapes=[tokens_vmem, tokens_vmem, pltpu.SemaphoreType.DMA((2 * CHUNKS,))],
        compiler_params=limit(8),
        cost_estimate=pl.CostEstimate(flops=2 * tokens * extent * extent, bytes_accessed=2**20, transcendentals=0),
        name="grad_part",
    )(in_hbm(x_in), in_hbm(grad_out))
    z_size = groups // Y_LO
    order = [list(range(z_size // 2)), list(range(z_size - 1, z_size // 2 - 1, -1))]
    halves = [[z * Y_LO + y for z in zs for y in range(Y_LO)] for zs in order]
    members = len(halves[0])
    received = exchange(grad_part, halves)
    layer_part, input_part = pl.pallas_call(
        outputs_kernel,
        out_shape=[whole, whole],
        in_specs=[HBM, HBM, HBM, ANY],
        out_specs=[VMEM, VMEM],
        scratch_shapes=[
            tokens_vmem,
            tokens_vmem,
            pltpu.VMEM((extent, extent), BF16),
            pltpu.SemaphoreType.DMA((3 * CHUNKS,)),
        ],
        compiler_params=limit(8),
        cost_estimate=pl.CostEstimate(flops=4 * tokens * extent * extent, bytes_accessed=2**20, transcendentals=0),
        name="outputs_part",
    )(x_in, grad_out, weight, grad_part)
    layer_near = partner(layer_part, "precond", 1)
    half, input_sum = pl.pallas_call(
        functools.partial(sum_kernel, members),
        out_shape=[pltpu.VMEM((extent // members, extent), BF16), whole],
        in_specs=[VMEM, VMEM, VMEM, ANY],
        out_specs=[VMEM] * 2,
        compiler_params=limit(8),
        cost_estimate=pl.CostEstimate(flops=extent * extent, bytes_accessed=2**20, transcendentals=0),
        name="sums",
    )(received, input_part, partner(input_part, "tensor", 1), layer_near)
    across = [pair for a, b in zip(*halves) for pair in ((a, b), (b, a))]
    copies = pl.pallas_call(
        copies_kernel,
        out_shape=block,
        in_specs=[VMEM, VMEM],
        out_specs=VMEM,
        compiler_params=limit(8),
        cost_estimate=pl.CostEstimate(flops=extent * extent, bytes_accessed=2**19, transcendentals=0),
        name="copies",
    )(half, lax.ppermute(half, "dp", across))
    grad_low = exchange(copies, halves)

    grad_in, layer_sum = pl.pallas_call(
        middle_kernel,
        out_shape=[whole, whole],
        in_specs=[VMEM] * 4,
        out_specs=[VMEM] * 2,
        compiler_params=limit(8),
        cost_estimate=pl.CostEstimate(flops=0, bytes_accessed=2**19, transcendentals=0),
        name="middle",
    )(input_sum, partner(input_sum, "tensor", 2), layer_part, layer_near)
    layer_other = partner(layer_sum, "precond", 2)

    root = jax.ShapeDtypeStruct((1, slab, extent), F32)
    left_near, right_near = pl.pallas_call(
        functools.partial(newton_kernel, slab),
        out_shape=[pltpu.VMEM((1, slab, extent), F32)] * 2,
        in_specs=[SMEM, VMEM],
        out_specs=[VMEM] * 2,
        scratch_shapes=[
            pltpu.VMEM((2, extent, extent), F32),
            pltpu.VMEM((2, 2, extent + slab, extent), BF16),
            pltpu.VMEM((2, extent, extent), BF16),
            pltpu.VMEM((2, extent, extent), BF16),
            pltpu.VMEM((2, slab, extent), F32),
        ],
        compiler_params=limit(24),
        cost_estimate=pl.CostEstimate(flops=0, bytes_accessed=2**16, transcendentals=0),
        name="newton",
    )(place, grad_low)
    layer_out, left_root, right_root = pl.pallas_call(
        last_kernel,
        out_shape=[whole, root, root],
        in_specs=[VMEM] * 4,
        out_specs=[VMEM] * 3,
        compiler_params=limit(8),
        cost_estimate=pl.CostEstimate(flops=0, bytes_accessed=2**18, transcendentals=0),
        name="last",
    )(layer_sum, layer_other, left_near, right_near)
    return layer_out, grad_in, left_root, right_root


def solution(mesh):
    in_specs = (P("dp", "precond"), P("dp", "tensor"), P("precond", "tensor"))
    out_specs = (
        P("dp", "tensor"),
        P("dp", "precond"),
        P("precond", "dp", "tensor"),
        P("precond", "dp", "tensor"),
    )
    return jax.shard_map(shards, mesh=mesh, in_specs=in_specs, out_specs=out_specs, check_vma=False)
```

```python
import functools

import jax
import jax.numpy as jnp
from jax import lax
from jax.experimental import pallas as pl
from jax.experimental.pallas import tpu as pltpu
from jax.sharding import PartitionSpec as P

ITERS = 6
VMEM = pl.BlockSpec(memory_space=pltpu.VMEM)
HBM = pl.BlockSpec(memory_space=pltpu.HBM)
ANY = pl.BlockSpec(memory_space=pl.ANY)
SMEM = pl.BlockSpec(memory_space=pltpu.SMEM)
F32 = jnp.float32
BF16 = jnp.bfloat16


def mm(left, right, dims=((1,), (0,))):
    return lax.dot_general(left, right, (dims, ((), ())), preferred_element_type=F32)


def fetch(sources, targets, sems):
    copies = [pltpu.make_async_copy(src, dst, sems.at[k]) for k, (src, dst) in enumerate(zip(sources, targets))]
    for copy in copies:
        copy.start()
    for copy in copies:
        copy.wait()


def grad_kernel(tokens_all, x_any, g_any, grad_ref, x_ref, g_ref, sems):
    fetch((x_any, g_any), (x_ref, g_ref), sems)
    grad = mm(x_ref[...], g_ref[...], ((0,), (0,)))
    grad_ref[...] = (grad * (1.0 / tokens_all)).astype(BF16)


def pair_sum(left_ref, right_ref):
    return (left_ref[...].astype(F32) + right_ref[...].astype(F32)).astype(BF16)


def sum_kernel(copies, parts_ref, input_ref, input_other, layer_any, out_ref, input_sum):
    slab = parts_ref.shape[0] // copies
    total = parts_ref[:slab, :].astype(F32)
    for k in range(1, copies):
        total = total + parts_ref[k * slab : (k + 1) * slab, :].astype(F32)
    total = total.astype(BF16)
    for k in range(copies):
        out_ref[k * slab : (k + 1) * slab, :] = total
    input_sum[...] = pair_sum(input_ref, input_other)


def outputs_kernel(x_any, g_any, w_any, after_any, layer_ref, input_ref, x_ref, g_ref, w_ref, sems):
    fetch((x_any, g_any, w_any), (x_ref, g_ref, w_ref), sems)
    layer_ref[...] = mm(x_ref[...], w_ref[...]).astype(BF16)
    input_ref[...] = mm(g_ref[...], w_ref[...], ((1,), (1,))).astype(BF16)


def middle_kernel(input_ref, input_other, layer_ref, layer_other, input_out, layer_sum):
    layer_sum[...] = pair_sum(layer_ref, layer_other)
    input_out[...] = pair_sum(input_ref, input_other)


def last_kernel(layer_ref, layer_other, left_ref, right_ref, layer_out, left_out, right_out):
    layer_out[...] = pair_sum(layer_ref, layer_other)
    left_out[...] = left_ref[...]
    right_out[...] = right_ref[...]


def staged(units):
    for product, use in units:
        use(product())


def newton_kernel(slab, place_ref, block_ref, left_ref, right_ref, wide, n_low, c_low, h_low, row):
    extent = block_ref.shape[0]
    half = extent // 2
    top, low = slice(0, half), slice(half, extent)
    sides = ((0, top), (0, low), (1, top), (1, low))
    first_row = pl.multiple_of(place_ref[0] * slab, slab)
    outs = (left_ref, right_ref)
    turned = h_low.at[1]
    turned[...] = block_ref[...].T
    on_diagonal = lax.broadcasted_iota(jnp.int32, (half, half), 0) == lax.broadcasted_iota(jnp.int32, (half, half), 1)
    own = first_row + lax.broadcasted_iota(jnp.int32, (slab, extent), 0)
    eye = jnp.where(own == lax.broadcasted_iota(jnp.int32, (slab, extent), 1), 1.25, 0.0)
    squares = [None, None]
    quarters = [None, None]

    def keep(ref, cut, values):
        values = values.astype(BF16)
        ref[cut.start : extent, cut] = values
        if cut == top:
            ref[top, low] = values[half:].T

    def gram(side, cut):
        if side == 0:
            return mm(block_ref[cut.start :, :], block_ref[cut, :], ((1,), (1,)))
        return mm(turned[cut.start :, :], block_ref[:, cut])

    def keep_gram(side, cut, product):
        corner = jnp.where(on_diagonal, product[:half] + 1e-06, product[:half])
        wide[side, cut, cut] = corner
        square = jnp.sum(corner * corner, axis=0, keepdims=True)
        if cut == top:
            below = product[half:]
            wide[side, low, top] = below
            wide[side, top, low] = below.T
            squares[side] = square + 2.0 * jnp.sum(below * below, axis=0, keepdims=True)
            return
        total = jnp.sum(squares[side] + square, axis=1, keepdims=True)
        scaling = 0.4 * jnp.sqrt(total + 1e-06)
        quarter = 0.25 / scaling
        quarters[side] = quarter
        n_low[side, 0, :extent, :] = (wide[side] * quarter).astype(BF16)
        start = 1.0 / jnp.sqrt(jnp.sqrt(scaling))
        first = start * (eye - quarter * wide[side, pl.ds(first_row, slab), :])
        row[side] = first
        n_low[side, 1, extent:, :] = first.astype(BF16)

    def unit(do, use, side, cut):
        return (lambda: do(side, cut)), (lambda product: use(side, cut, product))

    units = [unit(gram, keep_gram, *at) for at in sides]

    def square_n(now, riders, side, cut):
        return mm(n_low[side, now, cut.start : extent + riders, :], n_low[side, now, :extent, cut])

    def keep_c(now, riders, side, cut, product):
        scale = 2.5 * quarters[side] if now == 0 and riders == 0 else 2.5
        size = extent - cut.start
        keep(c_low.at[side], cut, product[:size] - scale * wide[side, cut.start :, cut])
        if riders:
            new = 1.25 * row[side, :, cut] - product[size:]
            row[side, :, cut] = new
            n_low[side, 1 - now, extent:, cut] = new.astype(BF16)

    def square_c(side, cut):
        return mm(c_low[side, cut.start :, :], c_low[side, :, cut])

    def keep_h(side, cut, product):
        keep(h_low.at[side], cut, 3.125 * c_low[side, cut.start :, cut].astype(F32) + product)

    def next_n(now, side, cut):
        return mm(h_low[side, cut.start :, :], n_low[side, now, :extent, cut])

    def keep_n(now, first, side, cut, product):
        scale = 2.44140625 * quarters[side] if first else 2.44140625
        n = scale * wide[side, cut.start :, cut] + product
        wide[side, cut.start :, cut] = n
        keep(n_low.at[side, 1 - now], cut, n)

    for k in range(ITERS - 2):
        now, riders = k % 2, (slab if k else 0)
        part = functools.partial
        units += [unit(part(square_n, now, riders), part(keep_c, now, riders), *at) for at in sides]
        units += [unit(square_c, keep_h, *at) for at in sides]
        units += [unit(part(next_n, now), part(keep_n, now, k == 0), *at) for at in sides]
    now = (ITERS - 2) % 2
    units += [unit(functools.partial(square_n, now, slab), functools.partial(keep_c, now, slab), *at) for at in sides]
    staged(units)

    ends = [row[side] for side in range(2)]
    for _ in range(2):
        for side in range(2):
            ends[side] = 1.5625 * ends[side] + mm(ends[side].astype(BF16), c_low[side])
    for side in range(2):
        outs[side][0] = 1.25 * row[side] - mm(ends[side].astype(BF16), n_low[side, now, :extent, :])


def in_hbm(values):
    return pltpu.with_memory_space_constraint(values, pltpu.HBM)


def limit(mebibytes):
    return pltpu.CompilerParams(vmem_limit_bytes=mebibytes * 2**20)


def exchange(values, axis):
    return lax.all_to_all(values, axis, 0, 0, tiled=True)


def partner(values, axis, flip):
    return lax.ppermute(values, axis, [(i, i ^ flip) for i in range(4)])


def shards(x_in, grad_out, weight):
    extent = weight.shape[0]
    tokens = x_in.shape[0]
    groups = lax.axis_size("dp")
    slab = extent // groups
    place = lax.axis_index("dp").astype(jnp.int32).reshape(1)
    block = pltpu.VMEM((extent, extent), BF16)
    whole = jax.ShapeDtypeStruct((tokens, extent), BF16)
    tokens_vmem = pltpu.VMEM((tokens, extent), BF16)

    grad_part = pl.pallas_call(
        functools.partial(grad_kernel, tokens * groups),
        out_shape=block,
        in_specs=[HBM, HBM],
        out_specs=VMEM,
        scratch_shapes=[tokens_vmem, tokens_vmem, pltpu.SemaphoreType.DMA((2,))],
        compiler_params=limit(8),
        cost_estimate=pl.CostEstimate(flops=2 * tokens * extent * extent, bytes_accessed=2**20, transcendentals=0),
        name="grad_part",
    )(in_hbm(x_in), in_hbm(grad_out))
    received = exchange(grad_part, "dp")
    layer_part, input_part = pl.pallas_call(
        outputs_kernel,
        out_shape=[whole, whole],
        in_specs=[HBM, HBM, HBM, ANY],
        out_specs=[VMEM, VMEM],
        scratch_shapes=[
            tokens_vmem,
            tokens_vmem,
            pltpu.VMEM((extent, extent), BF16),
            pltpu.SemaphoreType.DMA((3,)),
        ],
        compiler_params=limit(8),
        cost_estimate=pl.CostEstimate(flops=4 * tokens * extent * extent, bytes_accessed=2**20, transcendentals=0),
        name="outputs_part",
    )(x_in, grad_out, weight, grad_part)
    layer_near = partner(layer_part, "precond", 1)
    copies, input_sum = pl.pallas_call(
        functools.partial(sum_kernel, groups),
        out_shape=[block, whole],
        in_specs=[VMEM, VMEM, VMEM, ANY],
        out_specs=[VMEM] * 2,
        compiler_params=limit(8),
        cost_estimate=pl.CostEstimate(flops=extent * extent, bytes_accessed=2**20, transcendentals=0),
        name="sums",
    )(received, input_part, partner(input_part, "tensor", 1), layer_near)
    grad_low = exchange(copies, "dp")

    grad_in, layer_sum = pl.pallas_call(
        middle_kernel,
        out_shape=[whole, whole],
        in_specs=[VMEM] * 4,
        out_specs=[VMEM] * 2,
        compiler_params=limit(8),
        cost_estimate=pl.CostEstimate(flops=0, bytes_accessed=2**19, transcendentals=0),
        name="middle",
    )(input_sum, partner(input_sum, "tensor", 2), layer_part, layer_near)
    layer_other = partner(layer_sum, "precond", 2)

    root = jax.ShapeDtypeStruct((1, slab, extent), F32)
    left_near, right_near = pl.pallas_call(
        functools.partial(newton_kernel, slab),
        out_shape=[pltpu.VMEM((1, slab, extent), F32)] * 2,
        in_specs=[SMEM, VMEM],
        out_specs=[VMEM] * 2,
        scratch_shapes=[
            pltpu.VMEM((2, extent, extent), F32),
            pltpu.VMEM((2, 2, extent + slab, extent), BF16),
            pltpu.VMEM((2, extent, extent), BF16),
            pltpu.VMEM((2, extent, extent), BF16),
            pltpu.VMEM((2, slab, extent), F32),
        ],
        compiler_params=limit(24),
        cost_estimate=pl.CostEstimate(flops=0, bytes_accessed=2**16, transcendentals=0),
        name="newton",
    )(place, grad_low)
    layer_out, left_root, right_root = pl.pallas_call(
        last_kernel,
        out_shape=[whole, root, root],
        in_specs=[VMEM] * 4,
        out_specs=[VMEM] * 3,
        compiler_params=limit(8),
        cost_estimate=pl.CostEstimate(flops=0, bytes_accessed=2**18, transcendentals=0),
        name="last",
    )(layer_sum, layer_other, left_near, right_near)
    return layer_out, grad_in, left_root, right_root


def solution(mesh):
    in_specs = (P("dp", "precond"), P("dp", "tensor"), P("precond", "tensor"))
    out_specs = (
        P("dp", "tensor"),
        P("dp", "precond"),
        P("precond", "dp", "tensor"),
        P("precond", "dp", "tensor"),
    )
    return jax.shard_map(shards, mesh=mesh, in_specs=in_specs, out_specs=out_specs, check_vma=False)
```

```python
import functools

import jax
import jax.numpy as jnp
from jax import lax
from jax.experimental import pallas as pl
from jax.experimental.pallas import tpu as pltpu
from jax.sharding import PartitionSpec as P

ITERS = 6
VMEM = pl.BlockSpec(memory_space=pltpu.VMEM)
HBM = pl.BlockSpec(memory_space=pltpu.HBM)
ANY = pl.BlockSpec(memory_space=pl.ANY)
SMEM = pl.BlockSpec(memory_space=pltpu.SMEM)
F32 = jnp.float32
BF16 = jnp.bfloat16


def mm(left, right, dims=((1,), (0,))):
    return lax.dot_general(left, right, (dims, ((), ())), preferred_element_type=F32)


def fetch(sources, targets, sems):
    copies = [pltpu.make_async_copy(src, dst, sems.at[k]) for k, (src, dst) in enumerate(zip(sources, targets))]
    for copy in copies:
        copy.start()
    for copy in copies:
        copy.wait()


def products_kernel(
    tokens_all, x_any, g_any, w_any, grad_ref, layer_ref, input_ref, x_ref, g_ref, w_ref, sems
):
    fetch((x_any, g_any, w_any), (x_ref, g_ref, w_ref), sems)
    grad = mm(x_ref[...], g_ref[...], ((0,), (0,)))
    grad_ref[...] = (grad * (1.0 / tokens_all)).astype(BF16)
    layer_ref[...] = mm(x_ref[...], w_ref[...]).astype(BF16)
    input_ref[...] = mm(g_ref[...], w_ref[...], ((1,), (1,))).astype(BF16)


def hand_on_kernel(grad_ref, input_ref, layer_ref, after_ref, grad_out, input_out, layer_out):
    grad_out[...] = grad_ref[...]
    input_out[...] = input_ref[...]
    layer_out[...] = layer_ref[...]


def pair_sum(left_ref, right_ref):
    return (left_ref[...].astype(F32) + right_ref[...].astype(F32)).astype(BF16)


def sum_kernel(copies, parts_ref, input_ref, input_other, input_later, layer_any, out_ref, input_sum):
    slab = parts_ref.shape[0] // copies
    total = parts_ref[:slab, :].astype(F32)
    for k in range(1, copies):
        total = total + parts_ref[k * slab : (k + 1) * slab, :].astype(F32)
    total = total.astype(BF16)
    for k in range(copies):
        out_ref[k * slab : (k + 1) * slab, :] = total
    other = input_other[...].astype(F32) + input_later[...].astype(F32)
    input_sum[...] = (input_ref[...].astype(F32) + other).astype(BF16)


def middle_kernel(input_ref, input_other, layer_ref, layer_other, input_out, layer_sum):
    layer_sum[...] = pair_sum(layer_ref, layer_other)
    input_out[...] = pair_sum(input_ref, input_other)


def last_kernel(layer_ref, layer_other, left_ref, right_ref, layer_out, left_out, right_out):
    layer_out[...] = pair_sum(layer_ref, layer_other)
    left_out[...] = left_ref[...]
    right_out[...] = right_ref[...]


def staged(units):
    waiting = None
    for product, use in units:
        result = product()
        if waiting is not None:
            waiting[0](waiting[1])
        waiting = (use, result)
    waiting[0](waiting[1])


def newton_kernel(slab, place_ref, block_ref, left_ref, right_ref, wide, n_low, c_low, h_low, row):
    extent = block_ref.shape[0]
    half = extent // 2
    top, low = slice(0, half), slice(half, extent)
    sides = ((0, top), (0, low), (1, top), (1, low))
    first_row = pl.multiple_of(place_ref[0] * slab, slab)
    outs = (left_ref, right_ref)
    turned = h_low.at[1]
    turned[...] = block_ref[...].T
    on_diagonal = lax.broadcasted_iota(jnp.int32, (half, half), 0) == lax.broadcasted_iota(jnp.int32, (half, half), 1)
    own = first_row + lax.broadcasted_iota(jnp.int32, (slab, extent), 0)
    eye = jnp.where(own == lax.broadcasted_iota(jnp.int32, (slab, extent), 1), 1.25, 0.0)
    squares = [None, None]
    quarters = [None, None]

    def keep(ref, cut, values):
        values = values.astype(BF16)
        ref[cut.start : extent, cut] = values
        if cut == top:
            ref[top, low] = values[half:].T

    def gram(side, cut):
        left, right = (block_ref, turned) if side == 0 else (turned, block_ref)
        return mm(left[cut.start :, :], right[:, cut])

    def keep_gram(side, cut, product):
        corner = jnp.where(on_diagonal, product[:half] + 1e-06, product[:half])
        wide[side, cut, cut] = corner
        square = jnp.sum(corner * corner, axis=0, keepdims=True)
        if cut == top:
            below = product[half:]
            wide[side, low, top] = below
            wide[side, top, low] = below.T
            squares[side] = square + 2.0 * jnp.sum(below * below, axis=0, keepdims=True)
            return
        total = jnp.sum(squares[side] + square, axis=1, keepdims=True)
        scaling = 0.4 * jnp.sqrt(total + 1e-06)
        quarter = 0.25 / scaling
        quarters[side] = quarter
        n_low[side, 0, :extent, :] = (wide[side] * quarter).astype(BF16)
        start = 1.0 / jnp.sqrt(jnp.sqrt(scaling))
        first = start * (eye - quarter * wide[side, pl.ds(first_row, slab), :])
        row[side] = first
        n_low[side, 1, extent:, :] = first.astype(BF16)

    def unit(do, use, side, cut):
        return (lambda: do(side, cut)), (lambda product: use(side, cut, product))

    units = [unit(gram, keep_gram, *at) for at in sides]

    def square_n(now, riders, side, cut):
        return mm(n_low[side, now, cut.start : extent + riders, :], n_low[side, now, :extent, cut])

    def keep_c(now, riders, side, cut, product):
        scale = 2.5 * quarters[side] if now == 0 and riders == 0 else 2.5
        size = extent - cut.start
        keep(c_low.at[side], cut, product[:size] - scale * wide[side, cut.start :, cut])
        if riders:
            new = 1.25 * row[side, :, cut] - product[size:]
            row[side, :, cut] = new
            n_low[side, 1 - now, extent:, cut] = new.astype(BF16)

    def square_c(side, cut):
        return mm(c_low[side, cut.start :, :], c_low[side, :, cut])

    def keep_h(side, cut, product):
        keep(h_low.at[side], cut, 3.125 * c_low[side, cut.start :, cut].astype(F32) + product)

    def next_n(now, side, cut):
        return mm(h_low[side, cut.start :, :], n_low[side, now, :extent, cut])

    def keep_n(now, first, side, cut, product):
        scale = 2.44140625 * quarters[side] if first else 2.44140625
        n = scale * wide[side, cut.start :, cut] + product
        wide[side, cut.start :, cut] = n
        keep(n_low.at[side, 1 - now], cut, n)

    for k in range(ITERS - 2):
        now, riders = k % 2, (slab if k else 0)
        part = functools.partial
        units += [unit(part(square_n, now, riders), part(keep_c, now, riders), *at) for at in sides]
        units += [unit(square_c, keep_h, *at) for at in sides]
        units += [unit(part(next_n, now), part(keep_n, now, k == 0), *at) for at in sides]
    now = (ITERS - 2) % 2
    units += [unit(functools.partial(square_n, now, slab), functools.partial(keep_c, now, slab), *at) for at in sides]
    staged(units)

    ends = [row[side] for side in range(2)]
    for _ in range(2):
        for side in range(2):
            ends[side] = 1.5625 * ends[side] + mm(ends[side].astype(BF16), c_low[side])
    for side in range(2):
        outs[side][0] = 1.25 * row[side] - mm(ends[side].astype(BF16), n_low[side, now, :extent, :])


def in_hbm(values):
    return pltpu.with_memory_space_constraint(values, pltpu.HBM)


def limit(mebibytes):
    return pltpu.CompilerParams(vmem_limit_bytes=mebibytes * 2**20)


def exchange(values, axis):
    return lax.all_to_all(values, axis, 0, 0, tiled=True)


def partner(values, axis, flip):
    return lax.ppermute(values, axis, [(i, i ^ flip) for i in range(4)])


def core_partner(values, core):
    pairs = [(t * 4 + p, (t ^ 1) * 4 + p) for t in range(4) for p in (core, core + 2)]
    return lax.ppermute(values, ("tensor", "precond"), pairs)


def shards(x_in, grad_out, weight):
    extent = weight.shape[0]
    tokens = x_in.shape[0]
    groups = lax.axis_size("dp")
    slab = extent // groups
    place = lax.axis_index("dp").astype(jnp.int32).reshape(1)
    block = pltpu.VMEM((extent, extent), BF16)
    whole = jax.ShapeDtypeStruct((tokens, extent), BF16)
    tokens_vmem = pltpu.VMEM((tokens, extent), BF16)

    grad_near, layer_part, input_part = pl.pallas_call(
        functools.partial(products_kernel, tokens * groups),
        out_shape=[block, whole, whole],
        in_specs=[HBM, HBM, HBM],
        out_specs=[VMEM] * 3,
        scratch_shapes=[
            tokens_vmem,
            tokens_vmem,
            pltpu.VMEM((extent, extent), BF16),
            pltpu.SemaphoreType.DMA((3,)),
        ],
        compiler_params=limit(8),
        cost_estimate=pl.CostEstimate(flops=6 * tokens * extent * extent, bytes_accessed=2**20, transcendentals=0),
        name="products",
    )(in_hbm(x_in), in_hbm(grad_out), in_hbm(weight))
    input_other = core_partner(input_part, 0)
    grad_part, later_part, layer_part = pl.pallas_call(
        hand_on_kernel,
        out_shape=[jax.ShapeDtypeStruct((extent, extent), BF16), whole, whole],
        in_specs=[VMEM] * 4,
        out_specs=[VMEM] * 3,
        compiler_params=limit(8),
        cost_estimate=pl.CostEstimate(flops=0, bytes_accessed=2**20, transcendentals=0),
        name="hand_on",
    )(grad_near, input_part, layer_part, input_other)
    received = exchange(grad_part, "dp")
    layer_near = partner(layer_part, "precond", 1)
    copies, input_sum = pl.pallas_call(
        functools.partial(sum_kernel, groups),
        out_shape=[block, whole],
        in_specs=[VMEM, VMEM, VMEM, VMEM, ANY],
        out_specs=[VMEM] * 2,
        compiler_params=limit(8),
        cost_estimate=pl.CostEstimate(flops=extent * extent, bytes_accessed=2**20, transcendentals=0),
        name="sums",
    )(received, input_part, input_other, core_partner(later_part, 1), layer_near)
    grad_low = exchange(copies, "dp")

    grad_in, layer_sum = pl.pallas_call(
        middle_kernel,
        out_shape=[whole, whole],
        in_specs=[VMEM] * 4,
        out_specs=[VMEM] * 2,
        compiler_params=limit(8),
        cost_estimate=pl.CostEstimate(flops=0, bytes_accessed=2**19, transcendentals=0),
        name="middle",
    )(input_sum, partner(input_sum, "tensor", 2), layer_part, layer_near)
    layer_other = partner(layer_sum, "precond", 2)

    root = jax.ShapeDtypeStruct((1, slab, extent), F32)
    left_near, right_near = pl.pallas_call(
        functools.partial(newton_kernel, slab),
        out_shape=[pltpu.VMEM((1, slab, extent), F32)] * 2,
        in_specs=[SMEM, VMEM],
        out_specs=[VMEM] * 2,
        scratch_shapes=[
            pltpu.VMEM((2, extent, extent), F32),
            pltpu.VMEM((2, 2, extent + slab, extent), BF16),
            pltpu.VMEM((2, extent, extent), BF16),
            pltpu.VMEM((2, extent, extent), BF16),
            pltpu.VMEM((2, slab, extent), F32),
        ],
        compiler_params=limit(24),
        cost_estimate=pl.CostEstimate(flops=0, bytes_accessed=2**16, transcendentals=0),
        name="newton",
    )(place, grad_low)
    layer_out, left_root, right_root = pl.pallas_call(
        last_kernel,
        out_shape=[whole, root, root],
        in_specs=[VMEM] * 4,
        out_specs=[VMEM] * 3,
        compiler_params=limit(8),
        cost_estimate=pl.CostEstimate(flops=0, bytes_accessed=2**18, transcendentals=0),
        name="last",
    )(layer_sum, layer_other, left_near, right_near)
    return layer_out, grad_in, left_root, right_root


def solution(mesh):
    in_specs = (P("dp", "precond"), P("dp", "tensor"), P("precond", "tensor"))
    out_specs = (
        P("dp", "tensor"),
        P("dp", "precond"),
        P("precond", "dp", "tensor"),
        P("precond", "dp", "tensor"),
    )
    return jax.shard_map(shards, mesh=mesh, in_specs=in_specs, out_specs=out_specs, check_vma=False)
```

```python
import functools

import jax
import jax.numpy as jnp
from jax import lax
from jax.experimental import pallas as pl
from jax.experimental.pallas import tpu as pltpu
from jax.sharding import PartitionSpec as P

ITERS = 6
VMEM = pl.BlockSpec(memory_space=pltpu.VMEM)
HBM = pl.BlockSpec(memory_space=pltpu.HBM)
ANY = pl.BlockSpec(memory_space=pl.ANY)
SMEM = pl.BlockSpec(memory_space=pltpu.SMEM)
F32 = jnp.float32
BF16 = jnp.bfloat16


def mm(left, right, dims=((1,), (0,))):
    return lax.dot_general(left, right, (dims, ((), ())), preferred_element_type=F32)


def fetch(sources, targets, sems):
    copies = [pltpu.make_async_copy(src, dst, sems.at[k]) for k, (src, dst) in enumerate(zip(sources, targets))]
    for copy in copies:
        copy.start()
    for copy in copies:
        copy.wait()


def grad_kernel(tokens_all, x_any, g_any, grad_any, x_ref, g_ref, grad_ref, sems, out_sems):
    rows_in = x_ref.shape[0] // 4
    copies = []
    for source, target in ((x_any, x_ref), (g_any, g_ref)):
        for k in range(4):
            rows = slice(k * rows_in, (k + 1) * rows_in)
            copies.append(pltpu.make_async_copy(source.at[rows, :], target.at[rows, :], sems.at[len(copies)]))
    for copy in copies:
        copy.start()
    for copy in copies:
        copy.wait()
    outs = []
    chunk = grad_ref.shape[0] // 4
    for k in range(4):
        grad = mm(x_ref[:, k * chunk : (k + 1) * chunk], g_ref[...], ((0,), (0,)))
        grad_ref[k * chunk : (k + 1) * chunk, :] = (grad * (1.0 / tokens_all)).astype(BF16)
        for start in (k * chunk, k * chunk + chunk // 2):
            rows = slice(start, start + chunk // 2)
            outs.append(pltpu.make_async_copy(grad_ref.at[rows, :], grad_any.at[rows, :], out_sems.at[len(outs)]))
            outs[-1].start()
    for copy in outs:
        copy.wait()


def pair_sum(left_ref, right_ref):
    return (left_ref[...].astype(F32) + right_ref[...].astype(F32)).astype(BF16)


def sum_kernel(groups, parts_ref, input_ref, input_other, layer_any, out_any, input_sum, total_ref, sems):
    slab = parts_ref.shape[0] // groups
    total = parts_ref[:slab, :].astype(F32)
    for k in range(1, groups):
        total = total + parts_ref[k * slab : (k + 1) * slab, :].astype(F32)
    total = total.astype(BF16)
    block = total_ref.shape[0]
    for k in range(block // slab):
        total_ref[k * slab : (k + 1) * slab, :] = total
    copies = [
        pltpu.make_async_copy(total_ref, out_any.at[k * block : (k + 1) * block, :], sems.at[k])
        for k in range(out_any.shape[0] // block)
    ]
    for copy in copies:
        copy.start()
    input_sum[...] = pair_sum(input_ref, input_other)
    for copy in copies:
        copy.wait()


def outputs_kernel(x_any, g_any, w_any, after_any, layer_ref, input_ref, x_ref, g_ref, w_ref, sems):
    fetch((x_any, g_any, w_any), (x_ref, g_ref, w_ref), sems)
    layer_ref[...] = mm(x_ref[...], w_ref[...]).astype(BF16)
    input_ref[...] = mm(g_ref[...], w_ref[...], ((1,), (1,))).astype(BF16)


def middle_kernel(input_ref, input_other, layer_ref, layer_other, input_out, layer_sum):
    layer_sum[...] = pair_sum(layer_ref, layer_other)
    input_out[...] = pair_sum(input_ref, input_other)


def last_kernel(layer_ref, layer_other, left_ref, right_ref, layer_out, left_out, right_out):
    layer_out[...] = pair_sum(layer_ref, layer_other)
    left_out[...] = left_ref[...]
    right_out[...] = right_ref[...]


def staged(units):
    waiting = None
    for product, use in units:
        result = product()
        if waiting is not None:
            waiting[0](waiting[1])
        waiting = (use, result)
    waiting[0](waiting[1])


def newton_kernel(slab, place_ref, block_ref, left_ref, right_ref, wide, n_low, c_low, h_low, row):
    extent = block_ref.shape[0]
    half = extent // 2
    top, low = slice(0, half), slice(half, extent)
    sides = ((0, top), (0, low), (1, top), (1, low))
    first_row = pl.multiple_of(place_ref[0] * slab, slab)
    outs = (left_ref, right_ref)
    turned = h_low.at[1]
    turned[...] = block_ref[...].T
    on_diagonal = lax.broadcasted_iota(jnp.int32, (half, half), 0) == lax.broadcasted_iota(jnp.int32, (half, half), 1)
    own = first_row + lax.broadcasted_iota(jnp.int32, (slab, extent), 0)
    eye = jnp.where(own == lax.broadcasted_iota(jnp.int32, (slab, extent), 1), 1.25, 0.0)
    squares = [None, None]
    quarters = [None, None]

    def keep(ref, cut, values):
        values = values.astype(BF16)
        ref[cut.start : extent, cut] = values
        if cut == top:
            ref[top, low] = values[half:].T

    def gram(side, cut):
        left, right = (block_ref, turned) if side == 0 else (turned, block_ref)
        return mm(left[cut.start :, :], right[:, cut])

    def keep_gram(side, cut, product):
        corner = jnp.where(on_diagonal, product[:half] + 1e-06, product[:half])
        wide[side, cut, cut] = corner
        square = jnp.sum(corner * corner, axis=0, keepdims=True)
        if cut == top:
            below = product[half:]
            wide[side, low, top] = below
            wide[side, top, low] = below.T
            squares[side] = square + 2.0 * jnp.sum(below * below, axis=0, keepdims=True)
            return
        total = jnp.sum(squares[side] + square, axis=1, keepdims=True)
        scaling = 0.4 * jnp.sqrt(total + 1e-06)
        quarter = 0.25 / scaling
        quarters[side] = quarter
        n_low[side, 0, :extent, :] = (wide[side] * quarter).astype(BF16)
        start = 1.0 / jnp.sqrt(jnp.sqrt(scaling))
        first = start * (eye - quarter * wide[side, pl.ds(first_row, slab), :])
        row[side] = first
        n_low[side, 1, extent:, :] = first.astype(BF16)

    def unit(do, use, side, cut):
        return (lambda: do(side, cut)), (lambda product: use(side, cut, product))

    units = [unit(gram, keep_gram, *at) for at in sides]

    def square_n(now, riders, side, cut):
        return mm(n_low[side, now, cut.start : extent + riders, :], n_low[side, now, :extent, cut])

    def keep_c(now, riders, side, cut, product):
        scale = 2.5 * quarters[side] if now == 0 and riders == 0 else 2.5
        size = extent - cut.start
        keep(c_low.at[side], cut, product[:size] - scale * wide[side, cut.start :, cut])
        if riders:
            new = 1.25 * row[side, :, cut] - product[size:]
            row[side, :, cut] = new
            n_low[side, 1 - now, extent:, cut] = new.astype(BF16)

    def square_c(side, cut):
        return mm(c_low[side, cut.start :, :], c_low[side, :, cut])

    def keep_h(side, cut, product):
        keep(h_low.at[side], cut, 3.125 * c_low[side, cut.start :, cut].astype(F32) + product)

    def next_n(now, side, cut):
        return mm(h_low[side, cut.start :, :], n_low[side, now, :extent, cut])

    def keep_n(now, first, side, cut, product):
        scale = 2.44140625 * quarters[side] if first else 2.44140625
        n = scale * wide[side, cut.start :, cut] + product
        wide[side, cut.start :, cut] = n
        keep(n_low.at[side, 1 - now], cut, n)

    for k in range(ITERS - 2):
        now, riders = k % 2, (slab if k else 0)
        part = functools.partial
        units += [unit(part(square_n, now, riders), part(keep_c, now, riders), *at) for at in sides]
        units += [unit(square_c, keep_h, *at) for at in sides]
        units += [unit(part(next_n, now), part(keep_n, now, k == 0), *at) for at in sides]
    now = (ITERS - 2) % 2
    units += [unit(functools.partial(square_n, now, slab), functools.partial(keep_c, now, slab), *at) for at in sides]
    staged(units)

    ends = [row[side] for side in range(2)]
    for _ in range(2):
        for side in range(2):
            ends[side] = 1.5625 * ends[side] + mm(ends[side].astype(BF16), c_low[side])
    for side in range(2):
        outs[side][0] = 1.25 * row[side] - mm(ends[side].astype(BF16), n_low[side, now, :extent, :])


def in_hbm(values):
    return pltpu.with_memory_space_constraint(values, pltpu.HBM)


def limit(mebibytes):
    return pltpu.CompilerParams(vmem_limit_bytes=mebibytes * 2**20)


def exchange(values, axis):
    return lax.all_to_all(values, axis, 0, 0, tiled=True)


def partner(values, axis, flip):
    return lax.ppermute(values, axis, [(i, i ^ flip) for i in range(4)])


def shards(x_in, grad_out, weight):
    extent = weight.shape[0]
    tokens = x_in.shape[0]
    groups = lax.axis_size("dp")
    slab = extent // groups
    place = lax.axis_index("dp").astype(jnp.int32).reshape(1)
    in_hbm_block = jax.ShapeDtypeStruct((extent, extent), BF16)
    whole = jax.ShapeDtypeStruct((tokens, extent), BF16)
    tokens_vmem = pltpu.VMEM((tokens, extent), BF16)

    grad_part = pl.pallas_call(
        functools.partial(grad_kernel, tokens * groups),
        out_shape=in_hbm_block,
        in_specs=[HBM, HBM],
        out_specs=HBM,
        scratch_shapes=[
            tokens_vmem,
            tokens_vmem,
            pltpu.VMEM((extent, extent), BF16),
            pltpu.SemaphoreType.DMA((8,)),
            pltpu.SemaphoreType.DMA((8,)),
        ],
        compiler_params=limit(8),
        cost_estimate=pl.CostEstimate(flops=2 * tokens * extent * extent, bytes_accessed=2**20, transcendentals=0),
        name="grad_part",
    )(in_hbm(x_in), in_hbm(grad_out))
    received = exchange(grad_part, "dp")
    layer_part, input_part = pl.pallas_call(
        outputs_kernel,
        out_shape=[whole, whole],
        in_specs=[HBM, HBM, HBM, ANY],
        out_specs=[VMEM, VMEM],
        scratch_shapes=[
            tokens_vmem,
            tokens_vmem,
            pltpu.VMEM((extent, extent), BF16),
            pltpu.SemaphoreType.DMA((3,)),
        ],
        compiler_params=limit(8),
        cost_estimate=pl.CostEstimate(flops=4 * tokens * extent * extent, bytes_accessed=2**20, transcendentals=0),
        name="outputs_part",
    )(x_in, grad_out, weight, grad_part)
    layer_near = partner(layer_part, "precond", 1)
    copies, input_sum = pl.pallas_call(
        functools.partial(sum_kernel, groups),
        out_shape=[in_hbm_block, whole],
        in_specs=[VMEM, VMEM, VMEM, ANY],
        out_specs=[HBM, VMEM],
        scratch_shapes=[pltpu.VMEM((extent // 8, extent), BF16), pltpu.SemaphoreType.DMA((8,))],
        compiler_params=limit(8),
        cost_estimate=pl.CostEstimate(flops=extent * extent, bytes_accessed=2**20, transcendentals=0),
        name="sums",
    )(received, input_part, partner(input_part, "tensor", 1), layer_near)
    grad_low = exchange(copies, "dp")

    grad_in, layer_sum = pl.pallas_call(
        middle_kernel,
        out_shape=[whole, whole],
        in_specs=[VMEM] * 4,
        out_specs=[VMEM] * 2,
        compiler_params=limit(8),
        cost_estimate=pl.CostEstimate(flops=0, bytes_accessed=2**19, transcendentals=0),
        name="middle",
    )(input_sum, partner(input_sum, "tensor", 2), layer_part, layer_near)
    layer_other = partner(layer_sum, "precond", 2)

    root = jax.ShapeDtypeStruct((1, slab, extent), F32)
    left_near, right_near = pl.pallas_call(
        functools.partial(newton_kernel, slab),
        out_shape=[pltpu.VMEM((1, slab, extent), F32)] * 2,
        in_specs=[SMEM, VMEM],
        out_specs=[VMEM] * 2,
        scratch_shapes=[
            pltpu.VMEM((2, extent, extent), F32),
            pltpu.VMEM((2, 2, extent + slab, extent), BF16),
            pltpu.VMEM((2, extent, extent), BF16),
            pltpu.VMEM((2, extent, extent), BF16),
            pltpu.VMEM((2, slab, extent), F32),
        ],
        compiler_params=limit(24),
        cost_estimate=pl.CostEstimate(flops=0, bytes_accessed=2**16, transcendentals=0),
        name="newton",
    )(place, grad_low)
    layer_out, left_root, right_root = pl.pallas_call(
        last_kernel,
        out_shape=[whole, root, root],
        in_specs=[VMEM] * 4,
        out_specs=[VMEM] * 3,
        compiler_params=limit(8),
        cost_estimate=pl.CostEstimate(flops=0, bytes_accessed=2**18, transcendentals=0),
        name="last",
    )(layer_sum, layer_other, left_near, right_near)
    return layer_out, grad_in, left_root, right_root


def solution(mesh):
    in_specs = (P("dp", "precond"), P("dp", "tensor"), P("precond", "tensor"))
    out_specs = (
        P("dp", "tensor"),
        P("dp", "precond"),
        P("precond", "dp", "tensor"),
        P("precond", "dp", "tensor"),
    )
    return jax.shard_map(shards, mesh=mesh, in_specs=in_specs, out_specs=out_specs, check_vma=False)
```

```python
import functools

import jax
import jax.numpy as jnp
from jax import lax
from jax.experimental import pallas as pl
from jax.experimental.pallas import tpu as pltpu
from jax.sharding import PartitionSpec as P

ITERS = 6
ORDER = (
    (26, 6, 9, 23, 12, 28, 25, 22, 15, 31, 5, 24, 4, 17, 18, 27)
    + (13, 20, 10, 7, 30, 16, 19, 8, 2, 1, 21, 3, 11, 29, 0, 14)
)
VMEM = pl.BlockSpec(memory_space=pltpu.VMEM)
HBM = pl.BlockSpec(memory_space=pltpu.HBM)
ANY = pl.BlockSpec(memory_space=pl.ANY)
SMEM = pl.BlockSpec(memory_space=pltpu.SMEM)
F32 = jnp.float32
BF16 = jnp.bfloat16


def mm(left, right, dims=((1,), (0,))):
    return lax.dot_general(left, right, (dims, ((), ())), preferred_element_type=F32)


def fetch(sources, targets, sems):
    copies = [pltpu.make_async_copy(src, dst, sems.at[k]) for k, (src, dst) in enumerate(zip(sources, targets))]
    for copy in copies:
        copy.start()
    for copy in copies:
        copy.wait()


def grad_kernel(tokens_all, x_any, g_any, grad_ref, x_ref, g_ref, sems):
    fetch((x_any, g_any), (x_ref, g_ref), sems)
    grad = mm(x_ref[...], g_ref[...], ((0,), (0,)))
    grad_ref[...] = (grad * (1.0 / tokens_all)).astype(BF16)


def pair_sum(left_ref, right_ref):
    return (left_ref[...].astype(F32) + right_ref[...].astype(F32)).astype(BF16)


def sum_kernel(copies, parts_ref, input_ref, input_other, layer_any, out_ref, input_sum):
    slab = parts_ref.shape[0] // copies
    total = parts_ref[:slab, :].astype(F32)
    for k in range(1, copies):
        total = total + parts_ref[k * slab : (k + 1) * slab, :].astype(F32)
    total = total.astype(BF16)
    for k in range(copies):
        out_ref[k * slab : (k + 1) * slab, :] = total
    input_sum[...] = pair_sum(input_ref, input_other)


def outputs_kernel(x_any, g_any, w_any, after_any, layer_ref, input_ref, x_ref, g_ref, w_ref, sems):
    fetch((x_any, g_any, w_any), (x_ref, g_ref, w_ref), sems)
    layer_ref[...] = mm(x_ref[...], w_ref[...]).astype(BF16)
    input_ref[...] = mm(g_ref[...], w_ref[...], ((1,), (1,))).astype(BF16)


def middle_kernel(input_ref, input_other, layer_ref, layer_other, input_out, layer_sum):
    layer_sum[...] = pair_sum(layer_ref, layer_other)
    input_out[...] = pair_sum(input_ref, input_other)


def last_kernel(layer_ref, layer_other, left_ref, right_ref, layer_out, left_out, right_out):
    layer_out[...] = pair_sum(layer_ref, layer_other)
    left_out[...] = left_ref[...]
    right_out[...] = right_ref[...]


def staged(units):
    waiting = None
    for product, use in units:
        result = product()
        if waiting is not None:
            waiting[0](waiting[1])
        waiting = (use, result)
    waiting[0](waiting[1])


def newton_kernel(slab, place_ref, block_ref, left_ref, right_ref, wide, n_low, c_low, h_low, row):
    extent = block_ref.shape[0]
    half = extent // 2
    top, low = slice(0, half), slice(half, extent)
    sides = ((0, top), (0, low), (1, top), (1, low))
    first_row = pl.multiple_of(place_ref[0] * slab, slab)
    outs = (left_ref, right_ref)
    turned = h_low.at[1]
    turned[...] = block_ref[...].T
    on_diagonal = lax.broadcasted_iota(jnp.int32, (half, half), 0) == lax.broadcasted_iota(jnp.int32, (half, half), 1)
    own = first_row + lax.broadcasted_iota(jnp.int32, (slab, extent), 0)
    eye = jnp.where(own == lax.broadcasted_iota(jnp.int32, (slab, extent), 1), 1.25, 0.0)
    squares = [None, None]
    quarters = [None, None]

    def keep(ref, cut, values):
        values = values.astype(BF16)
        ref[cut.start : extent, cut] = values
        if cut == top:
            ref[top, low] = values[half:].T

    def gram(side, cut):
        left, right = (block_ref, turned) if side == 0 else (turned, block_ref)
        return mm(left[cut.start :, :], right[:, cut])

    def keep_gram(side, cut, product):
        corner = jnp.where(on_diagonal, product[:half] + 1e-06, product[:half])
        wide[side, cut, cut] = corner
        square = jnp.sum(corner * corner, axis=0, keepdims=True)
        if cut == top:
            below = product[half:]
            wide[side, low, top] = below
            wide[side, top, low] = below.T
            squares[side] = square + 2.0 * jnp.sum(below * below, axis=0, keepdims=True)
            return
        total = jnp.sum(squares[side] + square, axis=1, keepdims=True)
        scaling = 0.4 * jnp.sqrt(total + 1e-06)
        quarter = 0.25 / scaling
        quarters[side] = quarter
        n_low[side, 0, :extent, :] = (wide[side] * quarter).astype(BF16)
        start = 1.0 / jnp.sqrt(jnp.sqrt(scaling))
        first = start * (eye - quarter * wide[side, pl.ds(first_row, slab), :])
        row[side] = first
        n_low[side, 1, extent:, :] = first.astype(BF16)

    def unit(do, use, side, cut):
        return (lambda: do(side, cut)), (lambda product: use(side, cut, product))

    units = [unit(gram, keep_gram, *at) for at in sides]

    def square_n(now, riders, side, cut):
        return mm(n_low[side, now, cut.start : extent + riders, :], n_low[side, now, :extent, cut])

    def keep_c(now, riders, side, cut, product):
        scale = 2.5 * quarters[side] if now == 0 and riders == 0 else 2.5
        size = extent - cut.start
        keep(c_low.at[side], cut, product[:size] - scale * wide[side, cut.start :, cut])
        if riders:
            new = 1.25 * row[side, :, cut] - product[size:]
            row[side, :, cut] = new
            n_low[side, 1 - now, extent:, cut] = new.astype(BF16)

    def square_c(side, cut):
        return mm(c_low[side, cut.start :, :], c_low[side, :, cut])

    def keep_h(side, cut, product):
        keep(h_low.at[side], cut, 3.125 * c_low[side, cut.start :, cut].astype(F32) + product)

    def next_n(now, side, cut):
        return mm(h_low[side, cut.start :, :], n_low[side, now, :extent, cut])

    def keep_n(now, first, side, cut, product):
        scale = 2.44140625 * quarters[side] if first else 2.44140625
        n = scale * wide[side, cut.start :, cut] + product
        wide[side, cut.start :, cut] = n
        keep(n_low.at[side, 1 - now], cut, n)

    for k in range(ITERS - 2):
        now, riders = k % 2, (slab if k else 0)
        part = functools.partial
        units += [unit(part(square_n, now, riders), part(keep_c, now, riders), *at) for at in sides]
        units += [unit(square_c, keep_h, *at) for at in sides]
        units += [unit(part(next_n, now), part(keep_n, now, k == 0), *at) for at in sides]
    now = (ITERS - 2) % 2
    units += [unit(functools.partial(square_n, now, slab), functools.partial(keep_c, now, slab), *at) for at in sides]
    staged(units)

    ends = [row[side] for side in range(2)]
    for _ in range(2):
        for side in range(2):
            ends[side] = 1.5625 * ends[side] + mm(ends[side].astype(BF16), c_low[side])
    for side in range(2):
        outs[side][0] = 1.25 * row[side] - mm(ends[side].astype(BF16), n_low[side, now, :extent, :])


def in_hbm(values):
    return pltpu.with_memory_space_constraint(values, pltpu.HBM)


def limit(mebibytes):
    return pltpu.CompilerParams(vmem_limit_bytes=mebibytes * 2**20)


def exchange(values):
    size = lax.axis_size("dp")
    order = ORDER if size == len(ORDER) else range(size)
    return lax.all_to_all(values, "dp", 0, 0, tiled=True, axis_index_groups=[list(order)])


def partner(values, axis, flip):
    return lax.ppermute(values, axis, [(i, i ^ flip) for i in range(4)])


def shards(x_in, grad_out, weight):
    extent = weight.shape[0]
    tokens = x_in.shape[0]
    groups = lax.axis_size("dp")
    slab = extent // groups
    place = lax.axis_index("dp").astype(jnp.int32).reshape(1)
    block = pltpu.VMEM((extent, extent), BF16)
    whole = jax.ShapeDtypeStruct((tokens, extent), BF16)
    tokens_vmem = pltpu.VMEM((tokens, extent), BF16)

    grad_part = pl.pallas_call(
        functools.partial(grad_kernel, tokens * groups),
        out_shape=block,
        in_specs=[HBM, HBM],
        out_specs=VMEM,
        scratch_shapes=[tokens_vmem, tokens_vmem, pltpu.SemaphoreType.DMA((2,))],
        compiler_params=limit(8),
        cost_estimate=pl.CostEstimate(flops=2 * tokens * extent * extent, bytes_accessed=2**20, transcendentals=0),
        name="grad_part",
    )(in_hbm(x_in), in_hbm(grad_out))
    received = exchange(grad_part)
    layer_part, input_part = pl.pallas_call(
        outputs_kernel,
        out_shape=[whole, whole],
        in_specs=[HBM, HBM, HBM, ANY],
        out_specs=[VMEM, VMEM],
        scratch_shapes=[
            tokens_vmem,
            tokens_vmem,
            pltpu.VMEM((extent, extent), BF16),
            pltpu.SemaphoreType.DMA((3,)),
        ],
        compiler_params=limit(8),
        cost_estimate=pl.CostEstimate(flops=4 * tokens * extent * extent, bytes_accessed=2**20, transcendentals=0),
        name="outputs_part",
    )(x_in, grad_out, weight, grad_part)
    layer_near = partner(layer_part, "precond", 1)
    copies, input_sum = pl.pallas_call(
        functools.partial(sum_kernel, groups),
        out_shape=[block, whole],
        in_specs=[VMEM, VMEM, VMEM, ANY],
        out_specs=[VMEM] * 2,
        compiler_params=limit(8),
        cost_estimate=pl.CostEstimate(flops=extent * extent, bytes_accessed=2**20, transcendentals=0),
        name="sums",
    )(received, input_part, partner(input_part, "tensor", 1), layer_near)
    grad_low = exchange(copies)

    grad_in, layer_sum = pl.pallas_call(
        middle_kernel,
        out_shape=[whole, whole],
        in_specs=[VMEM] * 4,
        out_specs=[VMEM] * 2,
        compiler_params=limit(8),
        cost_estimate=pl.CostEstimate(flops=0, bytes_accessed=2**19, transcendentals=0),
        name="middle",
    )(input_sum, partner(input_sum, "tensor", 2), layer_part, layer_near)
    layer_other = partner(layer_sum, "precond", 2)

    root = jax.ShapeDtypeStruct((1, slab, extent), F32)
    left_near, right_near = pl.pallas_call(
        functools.partial(newton_kernel, slab),
        out_shape=[pltpu.VMEM((1, slab, extent), F32)] * 2,
        in_specs=[SMEM, VMEM],
        out_specs=[VMEM] * 2,
        scratch_shapes=[
            pltpu.VMEM((2, extent, extent), F32),
            pltpu.VMEM((2, 2, extent + slab, extent), BF16),
            pltpu.VMEM((2, extent, extent), BF16),
            pltpu.VMEM((2, extent, extent), BF16),
            pltpu.VMEM((2, slab, extent), F32),
        ],
        compiler_params=limit(24),
        cost_estimate=pl.CostEstimate(flops=0, bytes_accessed=2**16, transcendentals=0),
        name="newton",
    )(place, grad_low)
    layer_out, left_root, right_root = pl.pallas_call(
        last_kernel,
        out_shape=[whole, root, root],
        in_specs=[VMEM] * 4,
        out_specs=[VMEM] * 3,
        compiler_params=limit(8),
        cost_estimate=pl.CostEstimate(flops=0, bytes_accessed=2**18, transcendentals=0),
        name="last",
    )(layer_sum, layer_other, left_near, right_near)
    return layer_out, grad_in, left_root, right_root


def solution(mesh):
    in_specs = (P("dp", "precond"), P("dp", "tensor"), P("precond", "tensor"))
    out_specs = (
        P("dp", "tensor"),
        P("dp", "precond"),
        P("precond", "dp", "tensor"),
        P("precond", "dp", "tensor"),
    )
    return jax.shard_map(shards, mesh=mesh, in_specs=in_specs, out_specs=out_specs, check_vma=False)
```

```python
import functools

import jax
import jax.numpy as jnp
from jax import lax
from jax.experimental import pallas as pl
from jax.experimental.pallas import tpu as pltpu
from jax.sharding import PartitionSpec as P

ITERS = 6
ORDER = (
    (26, 6, 9, 23, 12, 28, 25, 22, 15, 31, 5, 24, 4, 17, 18, 27)
    + (13, 20, 10, 7, 30, 16, 19, 8, 2, 1, 21, 3, 11, 29, 0, 14)
)
VMEM = pl.BlockSpec(memory_space=pltpu.VMEM)
HBM = pl.BlockSpec(memory_space=pltpu.HBM)
ANY = pl.BlockSpec(memory_space=pl.ANY)
SMEM = pl.BlockSpec(memory_space=pltpu.SMEM)
F32 = jnp.float32
BF16 = jnp.bfloat16


def mm(left, right, dims=((1,), (0,))):
    return lax.dot_general(left, right, (dims, ((), ())), preferred_element_type=F32)


def fetch(sources, targets, sems):
    copies = [pltpu.make_async_copy(src, dst, sems.at[k]) for k, (src, dst) in enumerate(zip(sources, targets))]
    for copy in copies:
        copy.start()
    for copy in copies:
        copy.wait()


def grad_kernel(tokens_all, x_any, g_any, grad_ref, x_ref, g_ref, sems):
    fetch((x_any, g_any), (x_ref, g_ref), sems)
    grad = mm(x_ref[...], g_ref[...], ((0,), (0,)))
    grad_ref[...] = (grad * (1.0 / tokens_all)).astype(BF16)


def pair_sum(left_ref, right_ref):
    return (left_ref[...].astype(F32) + right_ref[...].astype(F32)).astype(BF16)


def sum_kernel(copies, parts_ref, input_ref, input_other, layer_ref, layer_other, out_ref, input_sum, layer_sum):
    slab = parts_ref.shape[0] // copies
    total = parts_ref[:slab, :].astype(F32)
    for k in range(1, copies):
        total = total + parts_ref[k * slab : (k + 1) * slab, :].astype(F32)
    total = total.astype(BF16)
    for k in range(copies):
        out_ref[k * slab : (k + 1) * slab, :] = total
    input_sum[...] = pair_sum(input_ref, input_other)
    layer_sum[...] = pair_sum(layer_ref, layer_other)


def outputs_kernel(x_any, g_any, w_any, after_any, layer_ref, input_ref, x_ref, g_ref, w_ref, sems):
    fetch((x_any, g_any, w_any), (x_ref, g_ref, w_ref), sems)
    layer_ref[...] = mm(x_ref[...], w_ref[...]).astype(BF16)
    input_ref[...] = mm(g_ref[...], w_ref[...], ((1,), (1,))).astype(BF16)


def middle_kernel(input_ref, input_other, input_out):
    input_out[...] = pair_sum(input_ref, input_other)


def last_kernel(layer_ref, layer_other, left_ref, right_ref, layer_out, left_out, right_out):
    layer_out[...] = pair_sum(layer_ref, layer_other)
    left_out[...] = left_ref[...]
    right_out[...] = right_ref[...]


def staged(units):
    waiting = None
    for product, use in units:
        result = product()
        if waiting is not None:
            waiting[0](waiting[1])
        waiting = (use, result)
    waiting[0](waiting[1])


def newton_kernel(slab, place_ref, block_ref, left_ref, right_ref, wide, n_low, c_low, h_low, row):
    extent = block_ref.shape[0]
    half = extent // 2
    top, low = slice(0, half), slice(half, extent)
    sides = ((0, top), (0, low), (1, top), (1, low))
    first_row = pl.multiple_of(place_ref[0] * slab, slab)
    outs = (left_ref, right_ref)
    turned = h_low.at[1]
    turned[...] = block_ref[...].T
    on_diagonal = lax.broadcasted_iota(jnp.int32, (half, half), 0) == lax.broadcasted_iota(jnp.int32, (half, half), 1)
    own = first_row + lax.broadcasted_iota(jnp.int32, (slab, extent), 0)
    eye = jnp.where(own == lax.broadcasted_iota(jnp.int32, (slab, extent), 1), 1.25, 0.0)
    squares = [None, None]
    quarters = [None, None]

    def keep(ref, cut, values):
        values = values.astype(BF16)
        ref[cut.start : extent, cut] = values
        if cut == top:
            ref[top, low] = values[half:].T

    def gram(side, cut):
        left, right = (block_ref, turned) if side == 0 else (turned, block_ref)
        return mm(left[cut.start :, :], right[:, cut])

    def keep_gram(side, cut, product):
        corner = jnp.where(on_diagonal, product[:half] + 1e-06, product[:half])
        wide[side, cut, cut] = corner
        square = jnp.sum(corner * corner, axis=0, keepdims=True)
        if cut == top:
            below = product[half:]
            wide[side, low, top] = below
            wide[side, top, low] = below.T
            squares[side] = square + 2.0 * jnp.sum(below * below, axis=0, keepdims=True)
            return
        total = jnp.sum(squares[side] + square, axis=1, keepdims=True)
        scaling = 0.4 * jnp.sqrt(total + 1e-06)
        quarter = 0.25 / scaling
        quarters[side] = quarter
        n_low[side, 0, :extent, :] = (wide[side] * quarter).astype(BF16)
        start = 1.0 / jnp.sqrt(jnp.sqrt(scaling))
        first = start * (eye - quarter * wide[side, pl.ds(first_row, slab), :])
        row[side] = first
        n_low[side, 1, extent:, :] = first.astype(BF16)

    def unit(do, use, side, cut):
        return (lambda: do(side, cut)), (lambda product: use(side, cut, product))

    units = [unit(gram, keep_gram, *at) for at in sides]

    def square_n(now, riders, side, cut):
        return mm(n_low[side, now, cut.start : extent + riders, :], n_low[side, now, :extent, cut])

    def keep_c(now, riders, side, cut, product):
        scale = 2.5 * quarters[side] if now == 0 and riders == 0 else 2.5
        size = extent - cut.start
        keep(c_low.at[side], cut, product[:size] - scale * wide[side, cut.start :, cut])
        if riders:
            new = 1.25 * row[side, :, cut] - product[size:]
            row[side, :, cut] = new
            n_low[side, 1 - now, extent:, cut] = new.astype(BF16)

    def square_c(side, cut):
        return mm(c_low[side, cut.start :, :], c_low[side, :, cut])

    def keep_h(side, cut, product):
        keep(h_low.at[side], cut, 3.125 * c_low[side, cut.start :, cut].astype(F32) + product)

    def next_n(now, side, cut):
        return mm(h_low[side, cut.start :, :], n_low[side, now, :extent, cut])

    def keep_n(now, first, side, cut, product):
        scale = 2.44140625 * quarters[side] if first else 2.44140625
        n = scale * wide[side, cut.start :, cut] + product
        wide[side, cut.start :, cut] = n
        keep(n_low.at[side, 1 - now], cut, n)

    for k in range(ITERS - 2):
        now, riders = k % 2, (slab if k else 0)
        part = functools.partial
        units += [unit(part(square_n, now, riders), part(keep_c, now, riders), *at) for at in sides]
        units += [unit(square_c, keep_h, *at) for at in sides]
        units += [unit(part(next_n, now), part(keep_n, now, k == 0), *at) for at in sides]
    now = (ITERS - 2) % 2
    units += [unit(functools.partial(square_n, now, slab), functools.partial(keep_c, now, slab), *at) for at in sides]
    staged(units)

    ends = [row[side] for side in range(2)]
    for _ in range(2):
        for side in range(2):
            ends[side] = 1.5625 * ends[side] + mm(ends[side].astype(BF16), c_low[side])
    for side in range(2):
        outs[side][0] = 1.25 * row[side] - mm(ends[side].astype(BF16), n_low[side, now, :extent, :])


def in_hbm(values):
    return pltpu.with_memory_space_constraint(values, pltpu.HBM)


def limit(mebibytes):
    return pltpu.CompilerParams(vmem_limit_bytes=mebibytes * 2**20)


def exchange(values):
    size = lax.axis_size("dp")
    order = ORDER if size == len(ORDER) else range(size)
    return lax.all_to_all(values, "dp", 0, 0, tiled=True, axis_index_groups=[list(order)])


def partner(values, axis, flip):
    return lax.ppermute(values, axis, [(i, i ^ flip) for i in range(4)])


def shards(x_in, grad_out, weight):
    extent = weight.shape[0]
    tokens = x_in.shape[0]
    groups = lax.axis_size("dp")
    slab = extent // groups
    place = lax.axis_index("dp").astype(jnp.int32).reshape(1)
    block = pltpu.VMEM((extent, extent), BF16)
    whole = jax.ShapeDtypeStruct((tokens, extent), BF16)
    tokens_vmem = pltpu.VMEM((tokens, extent), BF16)

    grad_part = pl.pallas_call(
        functools.partial(grad_kernel, tokens * groups),
        out_shape=block,
        in_specs=[HBM, HBM],
        out_specs=VMEM,
        scratch_shapes=[tokens_vmem, tokens_vmem, pltpu.SemaphoreType.DMA((2,))],
        compiler_params=limit(8),
        cost_estimate=pl.CostEstimate(flops=2 * tokens * extent * extent, bytes_accessed=2**20, transcendentals=0),
        name="grad_part",
    )(in_hbm(x_in), in_hbm(grad_out))
    received = exchange(grad_part)
    layer_part, input_part = pl.pallas_call(
        outputs_kernel,
        out_shape=[whole, whole],
        in_specs=[HBM, HBM, HBM, ANY],
        out_specs=[VMEM, VMEM],
        scratch_shapes=[
            tokens_vmem,
            tokens_vmem,
            pltpu.VMEM((extent, extent), BF16),
            pltpu.SemaphoreType.DMA((3,)),
        ],
        compiler_params=limit(8),
        cost_estimate=pl.CostEstimate(flops=4 * tokens * extent * extent, bytes_accessed=2**20, transcendentals=0),
        name="outputs_part",
    )(x_in, grad_out, weight, grad_part)
    layer_near = partner(layer_part, "precond", 1)
    copies, input_sum, layer_sum = pl.pallas_call(
        functools.partial(sum_kernel, groups),
        out_shape=[block, whole, whole],
        in_specs=[VMEM] * 5,
        out_specs=[VMEM] * 3,
        compiler_params=limit(8),
        cost_estimate=pl.CostEstimate(flops=extent * extent, bytes_accessed=2**20, transcendentals=0),
        name="sums",
    )(received, input_part, partner(input_part, "tensor", 1), layer_part, layer_near)
    grad_low = exchange(copies)

    grad_in = pl.pallas_call(
        middle_kernel,
        out_shape=whole,
        in_specs=[VMEM] * 2,
        out_specs=VMEM,
        compiler_params=limit(8),
        cost_estimate=pl.CostEstimate(flops=0, bytes_accessed=2**19, transcendentals=0),
        name="middle",
    )(input_sum, partner(input_sum, "tensor", 2))
    layer_other = partner(layer_sum, "precond", 2)

    root = jax.ShapeDtypeStruct((1, slab, extent), F32)
    left_near, right_near = pl.pallas_call(
        functools.partial(newton_kernel, slab),
        out_shape=[pltpu.VMEM((1, slab, extent), F32)] * 2,
        in_specs=[SMEM, VMEM],
        out_specs=[VMEM] * 2,
        scratch_shapes=[
            pltpu.VMEM((2, extent, extent), F32),
            pltpu.VMEM((2, 2, extent + slab, extent), BF16),
            pltpu.VMEM((2, extent, extent), BF16),
            pltpu.VMEM((2, extent, extent), BF16),
            pltpu.VMEM((2, slab, extent), F32),
        ],
        compiler_params=limit(24),
        cost_estimate=pl.CostEstimate(flops=0, bytes_accessed=2**16, transcendentals=0),
        name="newton",
    )(place, grad_low)
    layer_out, left_root, right_root = pl.pallas_call(
        last_kernel,
        out_shape=[whole, root, root],
        in_specs=[VMEM] * 4,
        out_specs=[VMEM] * 3,
        compiler_params=limit(8),
        cost_estimate=pl.CostEstimate(flops=0, bytes_accessed=2**18, transcendentals=0),
        name="last",
    )(layer_sum, layer_other, left_near, right_near)
    return layer_out, grad_in, left_root, right_root


def solution(mesh):
    in_specs = (P("dp", "precond"), P("dp", "tensor"), P("precond", "tensor"))
    out_specs = (
        P("dp", "tensor"),
        P("dp", "precond"),
        P("precond", "dp", "tensor"),
        P("precond", "dp", "tensor"),
    )
    return jax.shard_map(shards, mesh=mesh, in_specs=in_specs, out_specs=out_specs, check_vma=False)
```

```python
import functools

import jax
import jax.numpy as jnp
from jax import lax
from jax.experimental import pallas as pl
from jax.experimental.pallas import tpu as pltpu
from jax.sharding import PartitionSpec as P

ITERS = 6
ORDER = (
    (26, 6, 9, 23, 12, 28, 25, 22, 15, 31, 5, 24, 4, 17, 18, 27)
    + (13, 20, 10, 7, 30, 16, 19, 8, 2, 1, 21, 3, 11, 29, 0, 14)
)
VMEM = pl.BlockSpec(memory_space=pltpu.VMEM)
HBM = pl.BlockSpec(memory_space=pltpu.HBM)
ANY = pl.BlockSpec(memory_space=pl.ANY)
SMEM = pl.BlockSpec(memory_space=pltpu.SMEM)
F32 = jnp.float32
BF16 = jnp.bfloat16


def mm(left, right, dims=((1,), (0,))):
    return lax.dot_general(left, right, (dims, ((), ())), preferred_element_type=F32)


def fetch(sources, targets, sems):
    copies = [pltpu.make_async_copy(src, dst, sems.at[k]) for k, (src, dst) in enumerate(zip(sources, targets))]
    for copy in copies:
        copy.start()
    for copy in copies:
        copy.wait()


def grad_kernel(tokens_all, order, x_any, g_any, grad_ref, x_ref, g_ref, sems):
    fetch((x_any, g_any), (x_ref, g_ref), sems)
    grad = mm(x_ref[...], g_ref[...], ((0,), (0,)))
    low = (grad * (1.0 / tokens_all)).astype(BF16)
    slab = low.shape[0] // len(order)
    for j, owner in enumerate(order):
        grad_ref[j * slab : (j + 1) * slab, :] = low[owner * slab : (owner + 1) * slab, :]


def pair_sum(left_ref, right_ref):
    return (left_ref[...].astype(F32) + right_ref[...].astype(F32)).astype(BF16)


def sum_kernel(copies, parts_ref, input_ref, input_other, layer_any, out_ref, input_sum):
    slab = parts_ref.shape[0] // copies
    total = parts_ref[:slab, :].astype(F32)
    for k in range(1, copies):
        total = total + parts_ref[k * slab : (k + 1) * slab, :].astype(F32)
    total = total.astype(BF16)
    for k in range(copies):
        out_ref[k * slab : (k + 1) * slab, :] = total
    input_sum[...] = pair_sum(input_ref, input_other)


def outputs_kernel(x_any, g_any, w_any, after_any, layer_ref, input_ref, x_ref, g_ref, w_ref, sems):
    fetch((x_any, g_any, w_any), (x_ref, g_ref, w_ref), sems)
    layer_ref[...] = mm(x_ref[...], w_ref[...]).astype(BF16)
    input_ref[...] = mm(g_ref[...], w_ref[...], ((1,), (1,))).astype(BF16)


def middle_kernel(input_ref, input_other, layer_ref, layer_other, input_out, layer_sum):
    layer_sum[...] = pair_sum(layer_ref, layer_other)
    input_out[...] = pair_sum(input_ref, input_other)


def last_kernel(layer_ref, layer_other, left_ref, right_ref, layer_out, left_out, right_out):
    layer_out[...] = pair_sum(layer_ref, layer_other)
    left_out[...] = left_ref[...]
    right_out[...] = right_ref[...]


def staged(units):
    waiting = None
    for product, use in units:
        result = product()
        if waiting is not None:
            waiting[0](waiting[1])
        waiting = (use, result)
    waiting[0](waiting[1])


def newton_kernel(slab, place_ref, block_ref, left_ref, right_ref, wide, n_low, c_low, h_low, row):
    extent = block_ref.shape[0]
    half = extent // 2
    top, low = slice(0, half), slice(half, extent)
    sides = ((0, top), (0, low), (1, top), (1, low))
    first_row = pl.multiple_of(place_ref[0] * slab, slab)
    outs = (left_ref, right_ref)
    turned = h_low.at[1]
    turned[...] = block_ref[...].T
    on_diagonal = lax.broadcasted_iota(jnp.int32, (half, half), 0) == lax.broadcasted_iota(jnp.int32, (half, half), 1)
    own = first_row + lax.broadcasted_iota(jnp.int32, (slab, extent), 0)
    eye = jnp.where(own == lax.broadcasted_iota(jnp.int32, (slab, extent), 1), 1.25, 0.0)
    squares = [None, None]
    quarters = [None, None]

    def keep(ref, cut, values):
        values = values.astype(BF16)
        ref[cut.start : extent, cut] = values
        if cut == top:
            ref[top, low] = values[half:].T

    def gram(side, cut):
        left, right = (block_ref, turned) if side == 0 else (turned, block_ref)
        return mm(left[cut.start :, :], right[:, cut])

    def keep_gram(side, cut, product):
        corner = jnp.where(on_diagonal, product[:half] + 1e-06, product[:half])
        wide[side, cut, cut] = corner
        square = jnp.sum(corner * corner, axis=0, keepdims=True)
        if cut == top:
            below = product[half:]
            wide[side, low, top] = below
            wide[side, top, low] = below.T
            squares[side] = square + 2.0 * jnp.sum(below * below, axis=0, keepdims=True)
            return
        total = jnp.sum(squares[side] + square, axis=1, keepdims=True)
        scaling = 0.4 * jnp.sqrt(total + 1e-06)
        quarter = 0.25 / scaling
        quarters[side] = quarter
        n_low[side, 0, :extent, :] = (wide[side] * quarter).astype(BF16)
        start = 1.0 / jnp.sqrt(jnp.sqrt(scaling))
        first = start * (eye - quarter * wide[side, pl.ds(first_row, slab), :])
        row[side] = first
        n_low[side, 1, extent:, :] = first.astype(BF16)

    def unit(do, use, side, cut):
        return (lambda: do(side, cut)), (lambda product: use(side, cut, product))

    units = [unit(gram, keep_gram, *at) for at in sides]

    def square_n(now, riders, side, cut):
        return mm(n_low[side, now, cut.start : extent + riders, :], n_low[side, now, :extent, cut])

    def keep_c(now, riders, side, cut, product):
        scale = 2.5 * quarters[side] if now == 0 and riders == 0 else 2.5
        size = extent - cut.start
        keep(c_low.at[side], cut, product[:size] - scale * wide[side, cut.start :, cut])
        if riders:
            new = 1.25 * row[side, :, cut] - product[size:]
            row[side, :, cut] = new
            n_low[side, 1 - now, extent:, cut] = new.astype(BF16)

    def square_c(side, cut):
        return mm(c_low[side, cut.start :, :], c_low[side, :, cut])

    def keep_h(side, cut, product):
        keep(h_low.at[side], cut, 3.125 * c_low[side, cut.start :, cut].astype(F32) + product)

    def next_n(now, side, cut):
        return mm(h_low[side, cut.start :, :], n_low[side, now, :extent, cut])

    def keep_n(now, first, side, cut, product):
        scale = 2.44140625 * quarters[side] if first else 2.44140625
        n = scale * wide[side, cut.start :, cut] + product
        wide[side, cut.start :, cut] = n
        keep(n_low.at[side, 1 - now], cut, n)

    for k in range(ITERS - 2):
        now, riders = k % 2, (slab if k else 0)
        part = functools.partial
        units += [unit(part(square_n, now, riders), part(keep_c, now, riders), *at) for at in sides]
        units += [unit(square_c, keep_h, *at) for at in sides]
        units += [unit(part(next_n, now), part(keep_n, now, k == 0), *at) for at in sides]
    now = (ITERS - 2) % 2
    units += [unit(functools.partial(square_n, now, slab), functools.partial(keep_c, now, slab), *at) for at in sides]
    staged(units)

    ends = [row[side] for side in range(2)]
    for _ in range(2):
        for side in range(2):
            ends[side] = 1.5625 * ends[side] + mm(ends[side].astype(BF16), c_low[side])
    for side in range(2):
        outs[side][0] = 1.25 * row[side] - mm(ends[side].astype(BF16), n_low[side, now, :extent, :])


def in_hbm(values):
    return pltpu.with_memory_space_constraint(values, pltpu.HBM)


def limit(mebibytes):
    return pltpu.CompilerParams(vmem_limit_bytes=mebibytes * 2**20)


def exchange(values, order=None):
    groups = None if order is None else [list(order)]
    return lax.all_to_all(values, "dp", 0, 0, tiled=True, axis_index_groups=groups)


def partner(values, axis, flip):
    return lax.ppermute(values, axis, [(i, i ^ flip) for i in range(4)])


def shards(x_in, grad_out, weight):
    extent = weight.shape[0]
    tokens = x_in.shape[0]
    groups = lax.axis_size("dp")
    slab = extent // groups
    place = lax.axis_index("dp").astype(jnp.int32).reshape(1)
    block = pltpu.VMEM((extent, extent), BF16)
    whole = jax.ShapeDtypeStruct((tokens, extent), BF16)
    tokens_vmem = pltpu.VMEM((tokens, extent), BF16)

    order = ORDER if groups == len(ORDER) else tuple(range(groups))
    grad_part = pl.pallas_call(
        functools.partial(grad_kernel, tokens * groups, order),
        out_shape=block,
        in_specs=[HBM, HBM],
        out_specs=VMEM,
        scratch_shapes=[tokens_vmem, tokens_vmem, pltpu.SemaphoreType.DMA((2,))],
        compiler_params=limit(8),
        cost_estimate=pl.CostEstimate(flops=2 * tokens * extent * extent, bytes_accessed=2**20, transcendentals=0),
        name="grad_part",
    )(in_hbm(x_in), in_hbm(grad_out))
    received = exchange(grad_part, order)
    layer_part, input_part = pl.pallas_call(
        outputs_kernel,
        out_shape=[whole, whole],
        in_specs=[HBM, HBM, HBM, ANY],
        out_specs=[VMEM, VMEM],
        scratch_shapes=[
            tokens_vmem,
            tokens_vmem,
            pltpu.VMEM((extent, extent), BF16),
            pltpu.SemaphoreType.DMA((3,)),
        ],
        compiler_params=limit(8),
        cost_estimate=pl.CostEstimate(flops=4 * tokens * extent * extent, bytes_accessed=2**20, transcendentals=0),
        name="outputs_part",
    )(x_in, grad_out, weight, grad_part)
    layer_near = partner(layer_part, "precond", 1)
    copies, input_sum = pl.pallas_call(
        functools.partial(sum_kernel, groups),
        out_shape=[block, whole],
        in_specs=[VMEM, VMEM, VMEM, ANY],
        out_specs=[VMEM] * 2,
        compiler_params=limit(8),
        cost_estimate=pl.CostEstimate(flops=extent * extent, bytes_accessed=2**20, transcendentals=0),
        name="sums",
    )(received, input_part, partner(input_part, "tensor", 1), layer_near)
    grad_low = exchange(copies)

    grad_in, layer_sum = pl.pallas_call(
        middle_kernel,
        out_shape=[whole, whole],
        in_specs=[VMEM] * 4,
        out_specs=[VMEM] * 2,
        compiler_params=limit(8),
        cost_estimate=pl.CostEstimate(flops=0, bytes_accessed=2**19, transcendentals=0),
        name="middle",
    )(input_sum, partner(input_sum, "tensor", 2), layer_part, layer_near)
    layer_other = partner(layer_sum, "precond", 2)

    root = jax.ShapeDtypeStruct((1, slab, extent), F32)
    left_near, right_near = pl.pallas_call(
        functools.partial(newton_kernel, slab),
        out_shape=[pltpu.VMEM((1, slab, extent), F32)] * 2,
        in_specs=[SMEM, VMEM],
        out_specs=[VMEM] * 2,
        scratch_shapes=[
            pltpu.VMEM((2, extent, extent), F32),
            pltpu.VMEM((2, 2, extent + slab, extent), BF16),
            pltpu.VMEM((2, extent, extent), BF16),
            pltpu.VMEM((2, extent, extent), BF16),
            pltpu.VMEM((2, slab, extent), F32),
        ],
        compiler_params=limit(24),
        cost_estimate=pl.CostEstimate(flops=0, bytes_accessed=2**16, transcendentals=0),
        name="newton",
    )(place, grad_low)
    layer_out, left_root, right_root = pl.pallas_call(
        last_kernel,
        out_shape=[whole, root, root],
        in_specs=[VMEM] * 4,
        out_specs=[VMEM] * 3,
        compiler_params=limit(8),
        cost_estimate=pl.CostEstimate(flops=0, bytes_accessed=2**18, transcendentals=0),
        name="last",
    )(layer_sum, layer_other, left_near, right_near)
    return layer_out, grad_in, left_root, right_root


def solution(mesh):
    in_specs = (P("dp", "precond"), P("dp", "tensor"), P("precond", "tensor"))
    out_specs = (
        P("dp", "tensor"),
        P("dp", "precond"),
        P("precond", "dp", "tensor"),
        P("precond", "dp", "tensor"),
    )
    return jax.shard_map(shards, mesh=mesh, in_specs=in_specs, out_specs=out_specs, check_vma=False)
```
